128 devices in a mesh: ep: 32 (over y, z, core), tp: 4 (over x).
Axes of the slice: x: 4, y: 4, z: 4, core: 2. Of those that a mesh axis runs over, the one named last changes fastest.
Arguments:
- tokens: bfloat16 [4096, 4096], P('ep', 'tp'), may hold values from -6 to 6
- keep_mask: int32 [4096], P('ep'), may hold values 0 or 1
- expert_ids: int32 [4096, 8], P('ep'), may hold values from 0 to 63, all different within a row; in each aligned block of 128 rows (0 to 127, 128 to 255, ...) at most 32 rows name the same one
- route_weight: float32 [4096, 8], P('ep'), may hold values from 0.1 to 1
- w_gate: bfloat16 [64, 4096, 1536], P('ep', None, 'tp'), may hold values from -0.09375 to 0.09375
- w_up: bfloat16 [64, 4096, 1536], P('ep', None, 'tp'), may hold values from -0.09375 to 0.09375
- w_down: bfloat16 [64, 1536, 4096], P('ep', 'tp'), may hold values from -0.15625 to 0.15625
- norm_gain: float32 [4096], replicated, may hold values from 0.1 to 1.9
- kv_weight: bfloat16 [4096, 1024], P(None, 'tp'), may hold values from -0.09375 to 0.09375
Outputs:
- mixed_out: bfloat16 [4096, 4096], P('ep', 'tp')
- kv_rows: bfloat16 [4096, 1024], P('ep', 'tp')
The draws below stay inside these ranges and needn't reach their ends.
Inputs may be any that keep to these rules, and one draw needn't show every extreme that they name: `expert_ids`: within the rows of one device (128 rows, aligned blocks) no expert is named by more than 32 rows, a bound that some block reaches; a row names 8 different experts.
All inputs are finite; a program needn't handle non-finite values. No bound on the sum of `keep_mask` on one device may be relied on, other than what follows from the above.
Results may differ from the reference program's by a relative error of at most 0.014.
Values may be sent and summed in bfloat16 or wider, within the bound.
No kernel may reach another device: no remote copies, remote signals or barrier semaphores. Data moves between devices by JAX's collectives and lax.ppermute only.
A program may use at most 128 MiB of HBM per device.

```python
import math
import jax
import jax.numpy as jnp
import numpy as np
from jax import lax

D = 4096
FF = 1536
TOP = 8
TOK_DEV = 128
BLOCK = 128
EXPERTS = 64
TOKENS = 4096
CAP = 32
KVW = 1024
N_TP = 4


def touch_ends(entries, rng, smallest, high):
    shape = entries.shape
    index_at = [jax.random.randint(jax.random.fold_in(rng, axis), (), 0, shape[axis]) for axis in range(len(shape))]
    entries = entries.at[tuple(index_at)].set(smallest)
    longest = shape.index(max(shape))
    index_at[longest] = (index_at[longest] + 1) % shape[longest]
    return entries.at[tuple(index_at)].set(high)


def level_of(own_key, shape, cuts, smallest, top_value):
    level, own = 1.0, jax.random.fold_in(own_key, 6)
    for axis_at, shards_of in cuts:
        draws = jnp.exp(jax.random.uniform(jax.random.fold_in(own, axis_at), (shards_of,), jnp.float32, smallest / len(cuts), top_value / len(cuts)))
        level = level * jnp.repeat(draws, shape[axis_at] // shards_of).reshape([-1 if axis == axis_at else 1 for axis in range(len(shape))])
    return level


def routed_block(rng, own, number, rows, amount, top, reach, lean):
    order = jax.random.permutation(rng, amount)
    packed, common = load_shares(amount, rows * top, reach, lean, True), load_shares(amount, rows * top, reach, lean, False)
    places = jnp.arange(amount)

    def named(tallies, offset_by):
        used = int((tallies > 0).sum())
        fixed = max(1, used // 4)
        shifted = fixed + (places - fixed + offset_by * (used - fixed)) % max(1, amount - fixed)
        return jnp.zeros((amount,), jnp.int32).at[order[jnp.where(places < fixed, places, shifted)]].set(jnp.asarray(tallies, jnp.int32))

    tallies = jnp.where(number % 4 == 0, named(packed, number // 4), named(common, number - number // 4 - 1))
    mixed = jax.random.permutation(jax.random.fold_in(own, 3), amount)
    giver, receiver = mixed[0:amount // 2 * 2:2], mixed[1:amount // 2 * 2:2]
    margin = jnp.minimum(tallies[giver] - 1, reach - tallies[receiver]) // 2
    margin = jnp.where((giver == order[0]) | (receiver == order[0]) | (tallies[receiver] == 0), 0, jnp.maximum(margin, 0))
    shifted = jax.random.randint(jax.random.fold_in(own, 4), (amount // 2,), 0, 1 << 20) % (margin + 1)
    tallies = tallies.at[giver].add(-shifted).at[receiver].add(shifted)
    items = jnp.searchsorted(jnp.cumsum(tallies), jnp.arange(rows * top), side="right").astype(jnp.int32)
    listing = items.reshape(top, rows).T
    listing = listing[jax.random.permutation(jax.random.fold_in(own, 1), rows)]
    offset_by = jax.random.randint(jax.random.fold_in(own, 2), (rows, 1), 0, top)
    return jnp.take_along_axis(listing, (jnp.arange(top)[None, :] + offset_by) % top, axis=1)


def load_shares(number_of, total, most, lean, full):
    weights = [(1 << 20) // math.isqrt(standing ** lean) + 1 for standing in range(1, number_of + 1)]
    largest = most if full else min(most, max(-(-total // number_of), total * weights[0] // sum(weights)))
    least = 1 if total - largest >= number_of - 1 else 0
    given, rest = [largest] + [least] * (number_of - 1), total - largest - least * (number_of - 1)
    while rest > 0:
        movable = [i for i in range(1, number_of) if given[i] < largest] or [i for i in range(1, number_of) if given[i] < most]
        pool, left = sum([weights[i] for i in movable]), rest
        for i in movable:
            addition = min(most - given[i], max(1, left * weights[i] // pool), rest)
            given[i] = given[i] + addition
            rest = rest - addition
    return np.array(given)


def centred(stream_key, shape, spread, reach, split=(), held_as=jnp.bfloat16):
    loudness = level_of(stream_key, shape, split, -0.22, 0.18) if split else 1.0
    drawn = jax.random.normal(stream_key, shape, jnp.float32) * spread * loudness
    return jnp.minimum(jnp.maximum(drawn, -reach), reach).astype(held_as)


def setup_inputs(seed: int = 0) -> dict:
    streams_of = jax.random.split(jax.random.key(seed), 10)
    tokens = centred(streams_of[0], (TOKENS, D), 1.0, 6.0, ((0, 32), (1, 4)))
    keep_mask = touch_ends((jax.random.randint(streams_of[1], (TOKENS,), 0, 4) < 3).astype(jnp.int32), jax.random.fold_in(streams_of[1], 1), 0, 1)
    expert_ids_keys = jax.random.split(jax.random.fold_in(streams_of[2], 1), TOKENS // TOK_DEV)
    expert_ids_turns = jax.random.permutation(jax.random.fold_in(streams_of[2], 3), TOKENS // TOK_DEV)
    expert_ids = jax.vmap(lambda own, number: routed_block(jax.random.fold_in(streams_of[2], 2), own, number, TOK_DEV, EXPERTS, TOP, CAP, 2))(expert_ids_keys, expert_ids_turns).reshape((TOKENS, TOP))
    route_weight = jnp.clip(0.1 + 0.9 * jax.random.uniform(streams_of[3], (TOKENS, TOP), jnp.float32) ** level_of(streams_of[3], (TOKENS, TOP), ((0, 32),), -0.2, 0.2), 0.1, 1.0)
    w_gate = centred(streams_of[4], (EXPERTS, D, FF), D ** -0.5, 0.09375, ((0, 32), (2, 4)))
    w_up = centred(streams_of[5], (EXPERTS, D, FF), D ** -0.5, 0.09375, ((0, 32), (2, 4)))
    w_down = centred(streams_of[6], (EXPERTS, FF, D), FF ** -0.5, 0.15625, ((0, 32), (1, 4)))
    norm_gain = jnp.clip(1.0 + 0.18 * jax.random.normal(streams_of[7], (D,), jnp.float32), 0.1, 1.9)
    kv_weight = centred(streams_of[8], (D, KVW), D ** -0.5, 0.09375, ((1, 4),))
    return dict(tokens=tokens, keep_mask=keep_mask, expert_ids=expert_ids, route_weight=route_weight, w_gate=w_gate, w_up=w_up, w_down=w_down, norm_gain=norm_gain, kv_weight=kv_weight)


def reference(tokens, keep_mask, expert_ids, route_weight, w_gate, w_up, w_down, norm_gain, kv_weight):
    flat_expert = expert_ids.reshape(-1).astype(jnp.int32)
    active = jnp.repeat(keep_mask, TOP) > 0
    sort_keys = jnp.where(active, flat_expert, EXPERTS).astype(jnp.int32)
    route_order = jnp.argsort(sort_keys, stable=True).astype(jnp.int32)
    counts = lax.optimization_barrier(jnp.sum((sort_keys[:, None] == jnp.arange(EXPERTS, dtype=jnp.int32)[None, :]).astype(jnp.int32), axis=0))
    starts = jnp.cumsum(counts) - counts
    padded = (counts + BLOCK - 1) // BLOCK * BLOCK
    ending = jnp.cumsum(padded)
    opening = ending - padded
    flat_weight = route_weight.reshape(-1)
    quarter = FF // N_TP

    def visit(summed, block_idx):
        first = block_idx * BLOCK
        expert = jnp.sum((ending <= first).astype(jnp.int32))
        present = expert < EXPERTS
        chosen = jnp.minimum(expert, EXPERTS - 1)
        inside = first - opening[chosen] + jnp.arange(BLOCK, dtype=jnp.int32)
        usable = present & (inside < counts[chosen])
        route = route_order[jnp.clip(starts[chosen] + inside, 0, TOKENS * TOP - 1)]
        token_idx = route // TOP

        def expert_block(operand):
            row_data = tokens[token_idx]
            gate_val = jnp.dot(row_data, w_gate[chosen], preferred_element_type=jnp.float32)
            up_val = jnp.dot(row_data, w_up[chosen], preferred_element_type=jnp.float32)
            hidden = (jax.nn.silu(gate_val) * up_val).astype(jnp.bfloat16)
            pieces = jnp.einsum('rqf,qfd->qrd', hidden.reshape(BLOCK, N_TP, quarter).astype(jnp.float32), w_down[chosen].reshape(N_TP, quarter, D).astype(jnp.float32))
            pieces = lax.optimization_barrier(pieces.astype(jnp.bfloat16)).astype(jnp.float32)
            returned = lax.optimization_barrier(lax.optimization_barrier(jnp.sum(pieces, axis=0)).astype(jnp.bfloat16)).astype(jnp.float32)
            weights = jnp.where(usable, flat_weight[route], 0.0).astype(jnp.float32)
            return weights[:, None] * returned
        contrib = lax.cond(present, expert_block, lambda operand: jnp.zeros((BLOCK, D), jnp.float32), 0)
        return (summed.at[token_idx].add(contrib), None)
    nblocks = TOKENS * TOP // BLOCK + EXPERTS
    summed, unused = lax.scan(visit, jnp.zeros((TOKENS, D), jnp.float32), jnp.arange(nblocks, dtype=jnp.int32))
    mixed_out = (tokens.astype(jnp.float32) + summed).astype(jnp.bfloat16)
    full = mixed_out.astype(jnp.float32)
    mean_square = lax.optimization_barrier(jnp.mean(full * full, axis=-1, keepdims=True))
    normed = (full * lax.rsqrt(mean_square + 1e-06) * norm_gain).astype(jnp.bfloat16)
    kv_rows = jnp.dot(normed, kv_weight, preferred_element_type=jnp.float32).astype(jnp.bfloat16)
    return (mixed_out, kv_rows)
```

```python
import functools

import jax
import jax.numpy as jnp
import numpy as np
from jax import lax
from jax.experimental import pallas as pl
from jax.experimental.pallas import tpu as pltpu
from jax.sharding import Mesh, PartitionSpec as P

AXES = ("y", "z", "c", "x")
SIZES = (4, 4, 2, 4)
LINKS = (("x", 1), ("y", 3), ("z", 1), ("x", 3), ("y", 1), ("z", 3))
STAGES = len(LINKS)
PEERS = 1 << STAGES
HALF = PEERS // 2
BLOCKS = 16
TOK = 128
WIDTH = 1024
SLOTS = 32
CHIP_EXPERTS = 4
PART = (384, 384, 256)
OFFSET = (0, 384, 768)
PARTS = len(PART)


def link_of(part, core, stage):
    return LINKS[(2 * part + core + stage) % STAGES]


def device_number(at):
    return ((at["y"] * 4 + at["z"]) * 2 + at["c"]) * 4 + at["x"]


def all_places():
    for y in range(4):
        for z in range(4):
            for c in range(2):
                for x in range(4):
                    yield dict(y=y, z=z, c=c, x=x)


def stage_pairs(part, stage):
    pairs = []
    for at in all_places():
        axis, mask = link_of(part, at["c"], stage)
        to = dict(at)
        to[axis] ^= mask
        pairs.append((device_number(at), device_number(to)))
    return pairs


def core_pairs():
    return [(device_number(at), device_number(dict(at, c=1 - at["c"]))) for at in all_places()]


def x_pairs(mask):
    return [(device_number(at), device_number(dict(at, x=at["x"] ^ mask))) for at in all_places()]


def place_tables():
    place = np.zeros((128, PARTS, BLOCKS * 4), np.int32)
    owner = np.zeros((128, PARTS, PEERS), np.int32)
    for at in all_places():
        me = device_number(at)
        for part in range(PARTS):
            for j in range(PEERS):
                to = dict(at)
                for stage in range(STAGES):
                    if j >> stage & 1:
                        axis, mask = link_of(part, at["c"], stage)
                        to[axis] ^= mask
                code = (to["y"] * 4 + to["z"]) * 4 + to["x"]
                place[me, part, code] = j
                owner[me, part, j] = code
    return place.reshape(128, -1), owner.reshape(128, -1)


def gather_kernel(place, pick, lo0, hi0, lo1, hi1, lo2, hi2, out, rows, sems):
    block = pl.program_id(0)
    low, high = (lo0, lo1, lo2), (hi0, hi1, hi2)

    def fetch(which, slot, start):
        for x in range(4):
            for part in range(PARTS):
                to = rows.at[slot, :, pl.ds(x * WIDTH + OFFSET[part], PART[part])]
                sem = sems.at[slot, x * PARTS + part]
                if not start:
                    pltpu.make_async_copy(low[part].at[0], to, sem).wait()
                    continue
                j = place[part * PEERS + which * 4 + x]

                @pl.when(j < HALF)
                def _(part=part, j=j, to=to, sem=sem):
                    pltpu.make_async_copy(low[part].at[j], to, sem).start()

                @pl.when(j >= HALF)
                def _(part=part, j=j, to=to, sem=sem):
                    pltpu.make_async_copy(high[part].at[j - HALF], to, sem).start()

    @pl.when(block == 0)
    def _():
        fetch(0, 0, True)

    @pl.when(block + 1 < BLOCKS)
    def _():
        fetch(block + 1, lax.rem(block + 1, 2), True)

    slot = lax.rem(block, 2)
    fetch(block, slot, False)
    for x in range(4):
        cols = slice(x * WIDTH, (x + 1) * WIDTH)
        picked = jnp.dot(pick[0], rows[slot, :, cols], preferred_element_type=jnp.float32)
        picked = picked.astype(jnp.bfloat16)
        for e in range(CHIP_EXPERTS):
            out[e, 0, :, cols] = picked[e * SLOTS : (e + 1) * SLOTS]


def gather_rows(place, pick, pieces):
    flat = [half for pair in pieces for half in pair]
    return pl.pallas_call(
        gather_kernel,
        grid_spec=pltpu.PrefetchScalarGridSpec(
            num_scalar_prefetch=1,
            grid=(BLOCKS,),
            in_specs=[pl.BlockSpec((1, TOK, TOK), lambda b, t: (b, 0, 0))]
            + [pl.BlockSpec(memory_space=pl.ANY)] * 6,
            out_specs=pl.BlockSpec(
                (CHIP_EXPERTS, 1, SLOTS, 4 * WIDTH), lambda b, t: (0, b, 0, 0)
            ),
            scratch_shapes=[
                pltpu.VMEM((2, TOK, 4 * WIDTH), jnp.bfloat16),
                pltpu.SemaphoreType.DMA((2, 4 * PARTS)),
            ],
        ),
        out_shape=jax.ShapeDtypeStruct((CHIP_EXPERTS, BLOCKS, SLOTS, 4 * WIDTH), jnp.bfloat16),
        compiler_params=pltpu.CompilerParams(vmem_limit_bytes=24 << 20),
        cost_estimate=pl.CostEstimate(
            flops=2 * 2048 * 128 * 4096, bytes_accessed=34 << 20, transcendentals=0
        ),
        name="gather_rows",
    )(place, pick, *flat)


def expert_kernel(x, wg, wu, wd, weight, y0, y1, y2, gate, up):
    k = pl.program_id(1)
    g = jnp.dot(x[0], wg[0], preferred_element_type=jnp.float32)
    u = jnp.dot(x[0], wu[0], preferred_element_type=jnp.float32)

    @pl.when(k == 0)
    def _():
        gate[...] = g
        up[...] = u

    @pl.when(k > 0)
    def _():
        gate[...] += g
        up[...] += u

    @pl.when(k == 3)
    def _():
        hidden = (jax.nn.silu(gate[...]) * up[...] * weight[0]).astype(jnp.bfloat16)
        for s in range(4):
            cols = slice(s * WIDTH, (s + 1) * WIDTH)
            y = jnp.dot(hidden, wd[0, :, cols], preferred_element_type=jnp.float32)
            y = y.astype(jnp.bfloat16)
            for part, ref in enumerate((y0, y1, y2)):
                ref[0, s] = y[:, OFFSET[part] : OFFSET[part] + PART[part]]


def run_experts(rows, first, w_gate, w_up, w_down, weight):
    count, ff = w_gate.shape[0], w_gate.shape[2]
    n = BLOCKS * SLOTS
    return pl.pallas_call(
        expert_kernel,
        grid=(count, 4),
        in_specs=[
            pl.BlockSpec((1, n, WIDTH), lambda e, k: (e + first, 0, k)),
            pl.BlockSpec((1, WIDTH, ff), lambda e, k: (e, k, 0)),
            pl.BlockSpec((1, WIDTH, ff), lambda e, k: (e, k, 0)),
            pl.BlockSpec((1, ff, 4 * WIDTH), lambda e, k: (e, 0, 0)),
            pl.BlockSpec((1, n, 1), lambda e, k: (e + first, 0, 0)),
        ],
        out_specs=[pl.BlockSpec((1, 4, n, f), lambda e, k: (e, 0, 0, 0)) for f in PART],
        out_shape=[jax.ShapeDtypeStruct((count, 4, n, f), jnp.bfloat16) for f in PART],
        scratch_shapes=[pltpu.VMEM((n, ff), jnp.float32)] * 2,
        compiler_params=pltpu.CompilerParams(vmem_limit_bytes=48 << 20),
        cost_estimate=pl.CostEstimate(
            flops=2 * 2 * 512 * 4096 * 1152, bytes_accessed=36 << 20, transcendentals=512 * 768
        ),
        name="experts",
    )(rows, w_gate, w_up, w_down, weight)


def scatter_kernel(part, half, step, owner, put, ya, yb, out):
    first = half * HALF + pl.program_id(0) * step
    for i in range(step):
        code = owner[part * PEERS + first + i]
        block, x = lax.div(code, 4), lax.rem(code, 4)
        rows = pl.ds(pl.multiple_of(block * SLOTS, SLOTS), SLOTS)
        y = jnp.concatenate([ya[0, x, rows], ya[1, x, rows], yb[0, x, rows], yb[1, x, rows]], axis=0)
        out[i] = jnp.dot(put[block], y, preferred_element_type=jnp.float32).astype(jnp.bfloat16)


def scatter_rows(part, half, owner, put, ya, yb):
    f, step = PART[part], 8
    whole = pl.BlockSpec(ya.shape, lambda i, t: (0, 0, 0, 0))
    return pl.pallas_call(
        functools.partial(scatter_kernel, part, half, step),
        grid_spec=pltpu.PrefetchScalarGridSpec(
            num_scalar_prefetch=1,
            grid=(HALF // step,),
            in_specs=[pl.BlockSpec(put.shape, lambda i, t: (0, 0, 0)), whole, whole],
            out_specs=pl.BlockSpec((step, TOK, f), lambda i, t: (i, 0, 0)),
        ),
        out_shape=jax.ShapeDtypeStruct((HALF, TOK, f), jnp.bfloat16),
        compiler_params=pltpu.CompilerParams(vmem_limit_bytes=32 << 20),
        cost_estimate=pl.CostEstimate(
            flops=2 * 32 * 128 * 128 * f, bytes_accessed=10 << 20, transcendentals=0
        ),
        name="scatter_rows",
    )(owner, put, ya, yb)


def spread(piece, part):
    held = piece[None]
    for stage in range(STAGES):
        got = lax.ppermute(held, AXES, stage_pairs(part, stage))
        if stage < STAGES - 1:
            held = jnp.concatenate([held, got], axis=0)
    return held, got


def add(a, b):
    return (a.astype(jnp.float32) + b.astype(jnp.float32)).astype(jnp.bfloat16)


def collect(high, low, part):
    for stage in reversed(range(STAGES)):
        got = lax.ppermute(high, AXES, stage_pairs(part, stage))
        if stage:
            cut = 1 << (stage - 1)
            high, low = add(low[cut:], got[cut:]), add(low[:cut], got[:cut])
    return low[0].astype(jnp.float32) + got[0].astype(jnp.float32)


def on_device(
    tokens, keep_mask, expert_ids, route_weight, w_gate, w_up, w_down, norm_gain, kv_weight
):
    y, z, c, x = (lax.axis_index(a) for a in AXES)
    me = ((y * 4 + z) * 2 + c) * 4 + x
    place_all, owner_all = place_tables()
    place = lax.dynamic_index_in_dim(jnp.asarray(place_all), me, 0, keepdims=False)
    owner = lax.dynamic_index_in_dim(jnp.asarray(owner_all), me, 0, keepdims=False)

    experts = 2 * CHIP_EXPERTS * 8
    live = (keep_mask > 0)[:, None, None]
    named = expert_ids[:, :, None] == jnp.arange(experts, dtype=jnp.int32)
    routes = jnp.sum(jnp.where(named & live, route_weight[:, :, None], 0.0), axis=1)
    routes = lax.all_gather(routes, ("y", "z"), axis=0)

    other = [lax.ppermute(w, AXES, core_pairs()) for w in (w_gate, w_up, w_down)]
    pieces = [
        spread(tokens[:, OFFSET[p] : OFFSET[p] + PART[p]], p) for p in range(PARTS)
    ]

    chip = (y * 4 + z) * CHIP_EXPERTS
    mine = [
        lax.dynamic_slice_in_dim(routes, chip + 2 * who, 2, axis=2) for who in (c, 1 - c)
    ]
    mine = jnp.concatenate(mine, axis=2)
    marked = mine > 0
    until = jnp.asarray(np.tril(np.ones((TOK, TOK), np.float32)), jnp.bfloat16)
    rank = jnp.einsum(
        "ts,bse->bet", until, marked.astype(jnp.bfloat16), preferred_element_type=jnp.float32
    )
    rank = jnp.where(marked.transpose(0, 2, 1), rank.astype(jnp.int32) - 1, -1)
    onehot = rank[:, :, None, :] == jnp.arange(SLOTS, dtype=jnp.int32)[None, None, :, None]
    slot_weight = jnp.sum(jnp.where(onehot, mine.transpose(0, 2, 1)[:, :, None, :], 0.0), axis=3)
    slot_weight = slot_weight.transpose(1, 0, 2).reshape(CHIP_EXPERTS, BLOCKS * SLOTS, 1)
    pick = onehot.reshape(BLOCKS, TOK, TOK).astype(jnp.bfloat16)
    put = pick.transpose(0, 2, 1)

    rows = gather_rows(place, pick, pieces).reshape(CHIP_EXPERTS, BLOCKS * SLOTS, 4 * WIDTH)
    ya = run_experts(rows, 0, w_gate, w_up, w_down, slot_weight)
    yb = run_experts(rows, 2, *other, slot_weight)
    high = [scatter_rows(p, 1, owner, put, ya[p], yb[p]) for p in range(PARTS)]
    low = [scatter_rows(p, 0, owner, put, ya[p], yb[p]) for p in range(PARTS)]
    summed = jnp.concatenate([collect(high[p], low[p], p) for p in range(PARTS)], axis=1)
    mixed_out = (tokens.astype(jnp.float32) + summed).astype(jnp.bfloat16)

    full = [mixed_out] + [lax.ppermute(mixed_out, AXES, x_pairs(m)) for m in (1, 2, 3)]
    full = jnp.concatenate(full, axis=1).astype(jnp.float32)
    order = [jnp.bitwise_xor(x, m) * WIDTH for m in range(4)]
    gain = jnp.concatenate([lax.dynamic_slice_in_dim(norm_gain, o, WIDTH) for o in order])
    kv = jnp.concatenate([lax.dynamic_slice_in_dim(kv_weight, o, WIDTH) for o in order])
    mean_square = jnp.mean(full * full, axis=-1, keepdims=True)
    normed = (full * lax.rsqrt(mean_square + 1e-06) * gain).astype(jnp.bfloat16)
    kv_rows = jnp.dot(normed, kv, preferred_element_type=jnp.float32).astype(jnp.bfloat16)
    return (mixed_out, kv_rows)


def solution(mesh):
    fine = Mesh(mesh.devices.reshape(SIZES), AXES)
    ep = ("y", "z", "c")
    in_specs = (
        P(ep, "x"),
        P(ep),
        P(ep, None),
        P(ep, None),
        P(ep, None, "x"),
        P(ep, None, "x"),
        P(ep, "x", None),
        P(),
        P(None, "x"),
    )
    out_specs = (P(ep, "x"), P(ep, "x"))
    return jax.shard_map(
        on_device, mesh=fine, in_specs=in_specs, out_specs=out_specs, check_vma=False
    )
```

```python
import functools

import jax
import jax.numpy as jnp
import numpy as np
from jax import lax
from jax.experimental import pallas as pl
from jax.experimental.pallas import tpu as pltpu
from jax.sharding import Mesh, PartitionSpec as P

AXES = ("y", "z", "c", "x")
SIZES = (4, 4, 2, 4)
LINKS = (("x", 1), ("y", 3), ("z", 1), ("x", 3), ("y", 1), ("z", 3))
STAGES = len(LINKS)
PEERS = 1 << STAGES
HALF = PEERS // 2
BLOCKS = 16
TOK = 128
WIDTH = 1024
SLOTS = 32
CHIP_EXPERTS = 4
PART = (384, 384, 256)
OFFSET = (0, 384, 768)
PARTS = len(PART)
PAIRS = BLOCKS // 2
GROUPS = 4
SLOT_STEP = SLOTS // GROUPS
GROUP_ROWS = 2 * SLOT_STEP
TILE = PAIRS * GROUP_ROWS
PAIR_ROWS = CHIP_EXPERTS * GROUPS * GROUP_ROWS


def link_of(part, core, stage):
    return LINKS[(2 * part + core + stage) % STAGES]


def device_number(at):
    return ((at["y"] * 4 + at["z"]) * 2 + at["c"]) * 4 + at["x"]


def all_places():
    for y in range(4):
        for z in range(4):
            for c in range(2):
                for x in range(4):
                    yield dict(y=y, z=z, c=c, x=x)


def stage_pairs(part, stage):
    pairs = []
    for at in all_places():
        axis, mask = link_of(part, at["c"], stage)
        to = dict(at)
        to[axis] ^= mask
        pairs.append((device_number(at), device_number(to)))
    return pairs


def core_pairs():
    return [(device_number(at), device_number(dict(at, c=1 - at["c"]))) for at in all_places()]


def x_pairs(mask):
    return [(device_number(at), device_number(dict(at, x=at["x"] ^ mask))) for at in all_places()]


def place_tables():
    place = np.zeros((128, PARTS, BLOCKS * 4), np.int32)
    owner = np.zeros((128, PARTS, PEERS), np.int32)
    for at in all_places():
        me = device_number(at)
        for part in range(PARTS):
            for j in range(PEERS):
                to = dict(at)
                for stage in range(STAGES):
                    if j >> stage & 1:
                        axis, mask = link_of(part, at["c"], stage)
                        to[axis] ^= mask
                code = (to["y"] * 4 + to["z"]) * 4 + to["x"]
                place[me, part, code] = j
                owner[me, part, j] = code
    return place.reshape(128, -1), owner.reshape(128, -1)


def moe_kernel(
    place, groups, pick, weight, lo0, hi0, lo1, hi1, lo2, hi2, g_own, u_own, d_own, g_far, u_far, d_far,
    y0, y1, y2, rows, tok, wide, down, tok_sems, weight_sems, out_sems,
):
    low, high, outs = (lo0, lo1, lo2), (hi0, hi1, hi2), (y0, y1, y2)
    ff = g_own.shape[2]

    def weight_copies(e):
        slot, at = e % 2, e % 2
        gate, up, dn = (g_own, u_own, d_own) if e < 2 else (g_far, u_far, d_far)
        return (
            pltpu.make_async_copy(gate.at[at], wide.at[slot, :, pl.ds(0, ff)], weight_sems.at[slot, 0]),
            pltpu.make_async_copy(up.at[at], wide.at[slot, :, pl.ds(ff, ff)], weight_sems.at[slot, 1]),
            pltpu.make_async_copy(dn.at[at], down.at[slot], weight_sems.at[slot, 2]),
        )

    def fetch(pair, slot, start):
        for blk in range(2):
            for x in range(4):
                for part in range(PARTS):
                    to = tok.at[slot, pl.ds(blk * TOK, TOK), pl.ds(x * WIDTH + OFFSET[part], PART[part])]
                    sem = tok_sems.at[slot, (blk * 4 + x) * PARTS + part]
                    if not start:
                        pltpu.make_async_copy(low[part].at[0], to, sem).wait()
                        continue
                    j = place[part * PEERS + (2 * pair + blk) * 4 + x]

                    @pl.when(j < HALF)
                    def _(part=part, j=j, to=to, sem=sem):
                        pltpu.make_async_copy(low[part].at[j], to, sem).start()

                    @pl.when(j >= HALF)
                    def _(part=part, j=j, to=to, sem=sem):
                        pltpu.make_async_copy(high[part].at[j - HALF], to, sem).start()

    fetch(0, 0, True)
    for copy in weight_copies(0) + weight_copies(1):
        copy.start()

    @pl.loop(0, PAIRS)
    def _(pair):
        slot = lax.rem(pair, 2)

        @pl.when(pair + 1 < PAIRS)
        def _():
            fetch(pair + 1, 1 - slot, True)

        fetch(pair, slot, False)
        at = pl.multiple_of(pair * GROUP_ROWS, GROUP_ROWS)
        for x in range(4):
            cols = slice(x * WIDTH, (x + 1) * WIDTH)
            picked = jnp.dot(pick[pair], tok[slot, :, cols], preferred_element_type=jnp.float32)
            picked = picked.astype(jnp.bfloat16)
            for e in range(CHIP_EXPERTS):
                for g in range(GROUPS):
                    first = (e * GROUPS + g) * GROUP_ROWS
                    rows[e, pl.ds(g * TILE + at, GROUP_ROWS), cols] = picked[first : first + GROUP_ROWS]

    def out_copies(e):
        return [
            pltpu.make_async_copy(
                rows.at[e, :, pl.ds(x * WIDTH + OFFSET[part], PART[part])],
                outs[part].at[e, x],
                out_sems.at[e, x * PARTS + part],
            )
            for x in range(4)
            for part in range(PARTS)
        ]

    for e in range(CHIP_EXPERTS):
        slot = e % 2
        for copy in weight_copies(e):
            copy.wait()

        @pl.loop(0, groups[e])
        def _(g, e=e, slot=slot):
            tile = pl.ds(pl.multiple_of(g * TILE, TILE), TILE)
            both = jnp.dot(rows[e, tile, :], wide[slot], preferred_element_type=jnp.float32)
            hidden = jax.nn.silu(both[:, :ff]) * both[:, ff:] * weight[e, tile]
            hidden = hidden.astype(jnp.bfloat16)
            for x in range(4):
                cols = slice(x * WIDTH, (x + 1) * WIDTH)
                y = jnp.dot(hidden, down[slot, :, cols], preferred_element_type=jnp.float32)
                rows[e, tile, cols] = y.astype(jnp.bfloat16)

        if e + 2 < CHIP_EXPERTS:
            for copy in weight_copies(e + 2):
                copy.start()
        for copy in out_copies(e):
            copy.start()
    for e in range(CHIP_EXPERTS):
        for copy in out_copies(e):
            copy.wait()


def run_experts(place, groups, pick, weight, pieces, own, far):
    flat = [half for pair in pieces for half in pair]
    ff = own[0].shape[2]
    n = BLOCKS * SLOTS
    anywhere = pl.BlockSpec(memory_space=pl.ANY)
    vmem = pl.BlockSpec(memory_space=pltpu.VMEM)
    smem = pl.BlockSpec(memory_space=pltpu.SMEM)
    return pl.pallas_call(
        moe_kernel,
        in_specs=[smem, smem, vmem, vmem] + [anywhere] * 12,
        out_specs=[anywhere] * PARTS,
        out_shape=[jax.ShapeDtypeStruct((CHIP_EXPERTS, 4, n, f), jnp.bfloat16) for f in PART],
        scratch_shapes=[
            pltpu.VMEM((CHIP_EXPERTS, n, 4 * WIDTH), jnp.bfloat16),
            pltpu.VMEM((2, 2 * TOK, 4 * WIDTH), jnp.bfloat16),
            pltpu.VMEM((2, 4 * WIDTH, 2 * ff), jnp.bfloat16),
            pltpu.VMEM((2, ff, 4 * WIDTH), jnp.bfloat16),
            pltpu.SemaphoreType.DMA((2, 8 * PARTS)),
            pltpu.SemaphoreType.DMA((2, 3)),
            pltpu.SemaphoreType.DMA((CHIP_EXPERTS, 4 * PARTS)),
        ],
        compiler_params=pltpu.CompilerParams(vmem_limit_bytes=56 << 20),
        cost_estimate=pl.CostEstimate(
            flops=2 * 2048 * 4096 * 1408, bytes_accessed=72 << 20, transcendentals=2048 * 384
        ),
        name="experts",
    )(place, groups, pick, weight, *flat, *own, *far)


def scatter_kernel(part, half, step, owner, put, y, out):
    first = half * HALF + pl.program_id(0) * step
    for i in range(step):
        code = owner[part * PEERS + first + i]
        block, x = lax.div(code, 4), lax.rem(code, 4)
        at = pl.multiple_of(lax.div(block, 2) * GROUP_ROWS, GROUP_ROWS)
        terms = [
            y[e, x, pl.ds(g * TILE + at, GROUP_ROWS)] for e in range(CHIP_EXPERTS) for g in range(GROUPS)
        ]
        terms = jnp.concatenate(terms, axis=0)
        out[i] = jnp.dot(put[block], terms, preferred_element_type=jnp.float32).astype(jnp.bfloat16)


def scatter_rows(part, half, owner, put, y):
    f, step = PART[part], 8
    return pl.pallas_call(
        functools.partial(scatter_kernel, part, half, step),
        grid_spec=pltpu.PrefetchScalarGridSpec(
            num_scalar_prefetch=1,
            grid=(HALF // step,),
            in_specs=[
                pl.BlockSpec(put.shape, lambda i, t: (0, 0, 0)),
                pl.BlockSpec(y.shape, lambda i, t: (0, 0, 0, 0)),
            ],
            out_specs=pl.BlockSpec((step, TOK, f), lambda i, t: (i, 0, 0)),
        ),
        out_shape=jax.ShapeDtypeStruct((HALF, TOK, f), jnp.bfloat16),
        compiler_params=pltpu.CompilerParams(vmem_limit_bytes=32 << 20),
        cost_estimate=pl.CostEstimate(
            flops=2 * 32 * 128 * 256 * f, bytes_accessed=10 << 20, transcendentals=0
        ),
        name="scatter_rows",
    )(owner, put, y)


def spread(tokens, weights):
    held = [tokens[None, :, OFFSET[p] : OFFSET[p] + PART[p]] for p in range(PARTS)]
    weights, far = list(weights), []
    for stage in range(STAGES):
        if stage != 1 and len(far) < len(weights):
            far.append(lax.ppermute(weights[len(far)], AXES, core_pairs()))
        got = [lax.ppermute(held[p], AXES, stage_pairs(p, stage)) for p in range(PARTS)]
        if stage == STAGES - 1:
            return list(zip(held, got)), far
        held = [jnp.concatenate([h, g], axis=0) for h, g in zip(held, got)]
        if 1 <= stage <= 3:
            held, far, weights = lax.optimization_barrier((held, far, weights))


def add(a, b):
    return (a.astype(jnp.float32) + b.astype(jnp.float32)).astype(jnp.bfloat16)


def collect(high, low, part):
    for stage in reversed(range(STAGES)):
        got = lax.ppermute(high, AXES, stage_pairs(part, stage))
        if stage:
            cut = 1 << (stage - 1)
            high, low = add(low[cut:], got[cut:]), add(low[:cut], got[:cut])
    return low[0].astype(jnp.float32) + got[0].astype(jnp.float32)


def on_device(
    tokens, keep_mask, expert_ids, route_weight, w_gate, w_up, w_down, norm_gain, kv_weight
):
    y, z, c, x = (lax.axis_index(a) for a in AXES)
    me = ((y * 4 + z) * 2 + c) * 4 + x
    place_all, owner_all = place_tables()
    place = lax.dynamic_index_in_dim(jnp.asarray(place_all), me, 0, keepdims=False)
    owner = lax.dynamic_index_in_dim(jnp.asarray(owner_all), me, 0, keepdims=False)

    experts = CHIP_EXPERTS * BLOCKS
    live = (keep_mask > 0)[None, None, :]
    named = expert_ids.T[None] == jnp.arange(experts, dtype=jnp.int32)[:, None, None]
    routes = jnp.sum(jnp.where(named & live, route_weight.T[None], 0.0), axis=1)
    routes = routes.reshape(BLOCKS, CHIP_EXPERTS, TOK)
    routes = lax.all_to_all(routes, ("y", "z"), split_axis=0, concat_axis=0, tiled=True)
    own = (w_gate, w_up, w_down)
    pieces, far = spread(tokens, own)

    mine = jnp.where(c == 0, routes, jnp.concatenate([routes[:, 2:], routes[:, :2]], axis=1))
    marked = mine > 0
    until = jnp.asarray(np.triu(np.ones((TOK, TOK), np.float32)), jnp.bfloat16)
    rank = jnp.einsum(
        "bes,st->bet", marked.astype(jnp.bfloat16), until, preferred_element_type=jnp.float32
    )
    rank = jnp.where(marked, rank.astype(jnp.int32) - 1, -1)
    groups = jnp.max(rank, axis=(0, 2)) // SLOT_STEP + 1
    row = np.arange(GROUPS * GROUP_ROWS)
    row_slot = row // GROUP_ROWS * SLOT_STEP + row % SLOT_STEP
    row_block = row % GROUP_ROWS // SLOT_STEP
    same = jnp.asarray(row_block[:, None] == np.arange(2 * TOK)[None, :] // TOK)

    def by_pair(v):
        v = v.reshape(PAIRS, 2, CHIP_EXPERTS, TOK).transpose(0, 2, 1, 3)
        return v.reshape(PAIRS, CHIP_EXPERTS, 1, 2 * TOK)

    chosen = (by_pair(rank) == jnp.asarray(row_slot, jnp.int32)[:, None]) & same
    slot_weight = jnp.sum(jnp.where(chosen, by_pair(mine), 0.0), axis=3)
    slot_weight = slot_weight.reshape(PAIRS, CHIP_EXPERTS, GROUPS, GROUP_ROWS)
    slot_weight = slot_weight.transpose(1, 2, 0, 3).reshape(CHIP_EXPERTS, BLOCKS * SLOTS, 1)
    pick = chosen.astype(jnp.bfloat16).reshape(PAIRS, PAIR_ROWS, 2 * TOK)
    put = pick.reshape(PAIRS, PAIR_ROWS, 2, TOK).transpose(0, 2, 3, 1)
    put = put.reshape(BLOCKS, TOK, PAIR_ROWS)

    ys = run_experts(place, groups, pick, slot_weight, pieces, own, far)
    high = [scatter_rows(p, 1, owner, put, ys[p]) for p in range(PARTS)]
    low = [scatter_rows(p, 0, owner, put, ys[p]) for p in range(PARTS)]
    summed = jnp.concatenate([collect(high[p], low[p], p) for p in range(PARTS)], axis=1)
    mixed_out = (tokens.astype(jnp.float32) + summed).astype(jnp.bfloat16)

    full = [mixed_out] + [lax.ppermute(mixed_out, AXES, x_pairs(m)) for m in (1, 2, 3)]
    full = jnp.concatenate(full, axis=1).astype(jnp.float32)
    order = [jnp.bitwise_xor(x, m) * WIDTH for m in range(4)]
    gain = jnp.concatenate([lax.dynamic_slice_in_dim(norm_gain, o, WIDTH) for o in order])
    kv = jnp.concatenate([lax.dynamic_slice_in_dim(kv_weight, o, WIDTH) for o in order])
    mean_square = jnp.mean(full * full, axis=-1, keepdims=True)
    normed = (full * lax.rsqrt(mean_square + 1e-06) * gain).astype(jnp.bfloat16)
    kv_rows = jnp.dot(normed, kv, preferred_element_type=jnp.float32).astype(jnp.bfloat16)
    return (mixed_out, kv_rows)


def solution(mesh):
    fine = Mesh(mesh.devices.reshape(SIZES), AXES)
    ep = ("y", "z", "c")
    in_specs = (
        P(ep, "x"),
        P(ep),
        P(ep, None),
        P(ep, None),
        P(ep, None, "x"),
        P(ep, None, "x"),
        P(ep, "x", None),
        P(),
        P(None, "x"),
    )
    out_specs = (P(ep, "x"), P(ep, "x"))
    return jax.shard_map(
        on_device, mesh=fine, in_specs=in_specs, out_specs=out_specs, check_vma=False
    )
```

```python
import functools

import jax
import jax.numpy as jnp
import numpy as np
from jax import lax
from jax.experimental import pallas as pl
from jax.experimental.pallas import tpu as pltpu
from jax.sharding import Mesh, PartitionSpec as P

AXES = ("y", "z", "c", "x")
SIZES = (4, 4, 2, 4)
LINKS = (("x", 1), ("y", 3), ("z", 1), ("x", 3), ("y", 1), ("z", 3))
STAGES = len(LINKS)
PEERS = 1 << STAGES
HALF = PEERS // 2
BLOCKS = 16
TOK = 128
WIDTH = 1024
SLOTS = 32
CHIP_EXPERTS = 4
PART = (384, 384, 256)
OFFSET = (0, 384, 768)
PARTS = len(PART)
PAIRS = BLOCKS // 2
GROUPS = 4
SLOT_STEP = SLOTS // GROUPS
GROUP_ROWS = 2 * SLOT_STEP
TILE = PAIRS * GROUP_ROWS
SUM_STEP = 4
PAIR_ROWS = CHIP_EXPERTS * GROUPS * GROUP_ROWS


def link_of(part, core, stage):
    return LINKS[(2 * part + core + stage) % STAGES]


def device_number(at):
    return ((at["y"] * 4 + at["z"]) * 2 + at["c"]) * 4 + at["x"]


def all_places():
    for y in range(4):
        for z in range(4):
            for c in range(2):
                for x in range(4):
                    yield dict(y=y, z=z, c=c, x=x)


def stage_pairs(part, stage):
    pairs = []
    for at in all_places():
        axis, mask = link_of(part, at["c"], stage)
        to = dict(at)
        to[axis] ^= mask
        pairs.append((device_number(at), device_number(to)))
    return pairs


def core_pairs():
    return [(device_number(at), device_number(dict(at, c=1 - at["c"]))) for at in all_places()]


def x_pairs(mask):
    return [(device_number(at), device_number(dict(at, x=at["x"] ^ mask))) for at in all_places()]


def place_tables():
    place = np.zeros((128, PARTS, BLOCKS * 4), np.int32)
    owner = np.zeros((128, PARTS, PEERS), np.int32)
    for at in all_places():
        me = device_number(at)
        for part in range(PARTS):
            for j in range(PEERS):
                to = dict(at)
                for stage in range(STAGES):
                    if j >> stage & 1:
                        axis, mask = link_of(part, at["c"], stage)
                        to[axis] ^= mask
                code = (to["y"] * 4 + to["z"]) * 4 + to["x"]
                place[me, part, code] = j
                owner[me, part, j] = code
    return place.reshape(128, -1), owner.reshape(128, -1)


def moe_kernel(
    place, owner, groups, pick, put, weight, lo0, hi0, lo1, hi1, lo2, hi2, g_own, u_own, d_own, g_far, u_far, d_far,
    y0, y1, y2, s0, s1, s2, rows, tok, wide, down, sums, tok_sems, weight_sems, out_sems, sum_sems,
):
    low, high, outs, firsts = (lo0, lo1, lo2), (hi0, hi1, hi2), (y0, y1, y2), (s0, s1, s2)
    ff = g_own.shape[2]

    def weight_copies(e):
        slot, at = e % 2, e % 2
        gate, up, dn = (g_own, u_own, d_own) if e < 2 else (g_far, u_far, d_far)
        return (
            pltpu.make_async_copy(gate.at[at], wide.at[slot, :, pl.ds(0, ff)], weight_sems.at[slot, 0]),
            pltpu.make_async_copy(up.at[at], wide.at[slot, :, pl.ds(ff, ff)], weight_sems.at[slot, 1]),
            pltpu.make_async_copy(dn.at[at], down.at[slot], weight_sems.at[slot, 2]),
        )

    def fetch(pair, slot, start):
        for blk in range(2):
            for x in range(4):
                for part in range(PARTS):
                    to = tok.at[slot, pl.ds(blk * TOK, TOK), pl.ds(x * WIDTH + OFFSET[part], PART[part])]
                    sem = tok_sems.at[slot, (blk * 4 + x) * PARTS + part]
                    if not start:
                        pltpu.make_async_copy(low[part].at[0], to, sem).wait()
                        continue
                    j = place[part * PEERS + (2 * pair + blk) * 4 + x]

                    @pl.when(j < HALF)
                    def _(part=part, j=j, to=to, sem=sem):
                        pltpu.make_async_copy(low[part].at[j], to, sem).start()

                    @pl.when(j >= HALF)
                    def _(part=part, j=j, to=to, sem=sem):
                        pltpu.make_async_copy(high[part].at[j - HALF], to, sem).start()

    fetch(0, 0, True)
    for copy in weight_copies(0):
        copy.start()

    @pl.loop(0, PAIRS)
    def _(pair):
        slot = lax.rem(pair, 2)

        @pl.when(pair + 1 < PAIRS)
        def _():
            fetch(pair + 1, 1 - slot, True)

        fetch(pair, slot, False)
        at = pl.multiple_of(pair * GROUP_ROWS, GROUP_ROWS)
        for x in range(4):
            cols = slice(x * WIDTH, (x + 1) * WIDTH)
            picked = jnp.dot(pick[pair], tok[slot, :, cols], preferred_element_type=jnp.float32)
            picked = picked.astype(jnp.bfloat16)
            for e in range(CHIP_EXPERTS):
                for g in range(GROUPS):
                    first = (e * GROUPS + g) * GROUP_ROWS
                    rows[e, pl.ds(g * TILE + at, GROUP_ROWS), cols] = picked[first : first + GROUP_ROWS]

    def out_copies(e):
        return [
            pltpu.make_async_copy(
                rows.at[e, :, pl.ds(x * WIDTH + OFFSET[part], PART[part])],
                outs[part].at[e, x],
                out_sems.at[e, x * PARTS + part],
            )
            for x in range(4)
            for part in range(PARTS)
        ]

    for copy in weight_copies(1):
        copy.start()
    for e in range(CHIP_EXPERTS):
        slot = e % 2
        for copy in weight_copies(e):
            copy.wait()

        @pl.loop(0, lax.div(groups[e] + 1, 2))
        def _(g, e=e, slot=slot):
            tiles = [pl.ds(pl.multiple_of((2 * g + i) * TILE, TILE), TILE) for i in range(2)]
            hidden = []
            for tile in tiles:
                both = jnp.dot(rows[e, tile, :], wide[slot], preferred_element_type=jnp.float32)
                product = jax.nn.silu(both[:, :ff]) * both[:, ff:] * weight[e, tile]
                hidden.append(product.astype(jnp.bfloat16))
            for tile, left in zip(tiles, hidden):
                for x in range(4):
                    cols = slice(x * WIDTH, (x + 1) * WIDTH)
                    y = jnp.dot(left, down[slot, :, cols], preferred_element_type=jnp.float32)
                    rows[e, tile, cols] = y.astype(jnp.bfloat16)

        if e + 2 < CHIP_EXPERTS:
            for copy in weight_copies(e + 2):
                copy.start()
        for copy in out_copies(e):
            copy.start()

    for part in range(PARTS):
        f = PART[part]

        def send(i, slot, part=part, f=f):
            return pltpu.make_async_copy(
                sums.at[slot, :, :, pl.ds(0, f)],
                firsts[part].at[pl.ds(i * SUM_STEP, SUM_STEP)],
                sum_sems.at[slot],
            )

        @pl.loop(0, HALF // SUM_STEP)
        def _(i, part=part, f=f, send=send):
            slot = lax.rem(i, 2)

            @pl.when(i >= 2)
            def _():
                send(i - 2, slot).wait()

            for n in range(SUM_STEP):
                code = owner[part * PEERS + HALF + i * SUM_STEP + n]
                block, x = lax.div(code, 4), lax.rem(code, 4)
                at = pl.multiple_of(lax.div(block, 2) * GROUP_ROWS, GROUP_ROWS)
                cols = pl.ds(pl.multiple_of(x * WIDTH + OFFSET[part], 128), f)
                terms = [
                    rows[e, pl.ds(g * TILE + at, GROUP_ROWS), cols]
                    for e in range(CHIP_EXPERTS)
                    for g in range(GROUPS)
                ]
                terms = jnp.concatenate(terms, axis=0)
                total = jnp.dot(put[block], terms, preferred_element_type=jnp.float32)
                sums[slot, n, :, :f] = total.astype(jnp.bfloat16)
            send(i, slot).start()

        for i in (HALF // SUM_STEP - 2, HALF // SUM_STEP - 1):
            send(i, i % 2).wait()
    for e in range(CHIP_EXPERTS):
        for copy in out_copies(e):
            copy.wait()


def run_experts(place, owner, groups, pick, put, weight, pieces, own, far):
    flat = [half for pair in pieces for half in pair]
    ff = own[0].shape[2]
    n = BLOCKS * SLOTS
    anywhere = pl.BlockSpec(memory_space=pl.ANY)
    vmem = pl.BlockSpec(memory_space=pltpu.VMEM)
    smem = pl.BlockSpec(memory_space=pltpu.SMEM)
    return pl.pallas_call(
        moe_kernel,
        in_specs=[smem] * 3 + [vmem] * 3 + [anywhere] * 12,
        out_specs=[anywhere] * (2 * PARTS),
        out_shape=[jax.ShapeDtypeStruct((CHIP_EXPERTS, 4, n, f), jnp.bfloat16) for f in PART]
        + [jax.ShapeDtypeStruct((HALF, TOK, f), jnp.bfloat16) for f in PART],
        scratch_shapes=[
            pltpu.VMEM((CHIP_EXPERTS, n, 4 * WIDTH), jnp.bfloat16),
            pltpu.VMEM((2, 2 * TOK, 4 * WIDTH), jnp.bfloat16),
            pltpu.VMEM((2, 4 * WIDTH, 2 * ff), jnp.bfloat16),
            pltpu.VMEM((2, ff, 4 * WIDTH), jnp.bfloat16),
            pltpu.VMEM((2, SUM_STEP, TOK, max(PART)), jnp.bfloat16),
            pltpu.SemaphoreType.DMA((2, 8 * PARTS)),
            pltpu.SemaphoreType.DMA((2, 3)),
            pltpu.SemaphoreType.DMA((CHIP_EXPERTS, 4 * PARTS)),
            pltpu.SemaphoreType.DMA((2,)),
        ],
        compiler_params=pltpu.CompilerParams(vmem_limit_bytes=56 << 20),
        cost_estimate=pl.CostEstimate(
            flops=2 * 2048 * 4096 * 1664, bytes_accessed=80 << 20, transcendentals=2048 * 384
        ),
        name="experts",
    )(place, owner, groups, pick, put, weight, *flat, *own, *far)


def scatter_kernel(part, step, owner, put, y, out):
    first = pl.program_id(0) * step
    for i in range(step):
        code = owner[part * PEERS + first + i]
        block, x = lax.div(code, 4), lax.rem(code, 4)
        at = pl.multiple_of(lax.div(block, 2) * GROUP_ROWS, GROUP_ROWS)
        terms = [
            y[e, x, pl.ds(g * TILE + at, GROUP_ROWS)] for e in range(CHIP_EXPERTS) for g in range(GROUPS)
        ]
        terms = jnp.concatenate(terms, axis=0)
        out[i] = jnp.dot(put[block], terms, preferred_element_type=jnp.float32).astype(jnp.bfloat16)


def scatter_rows(part, owner, put, y):
    f, step = PART[part], 8
    return pl.pallas_call(
        functools.partial(scatter_kernel, part, step),
        grid_spec=pltpu.PrefetchScalarGridSpec(
            num_scalar_prefetch=1,
            grid=(HALF // step,),
            in_specs=[
                pl.BlockSpec(put.shape, lambda i, t: (0, 0, 0)),
                pl.BlockSpec(y.shape, lambda i, t: (0, 0, 0, 0)),
            ],
            out_specs=pl.BlockSpec((step, TOK, f), lambda i, t: (i, 0, 0)),
        ),
        out_shape=jax.ShapeDtypeStruct((HALF, TOK, f), jnp.bfloat16),
        compiler_params=pltpu.CompilerParams(vmem_limit_bytes=32 << 20),
        cost_estimate=pl.CostEstimate(
            flops=2 * 32 * 128 * 256 * f, bytes_accessed=10 << 20, transcendentals=0
        ),
        name="scatter_rows",
    )(owner, put, y)


def routing(routes, core):
    mine = jnp.where(core == 0, routes, jnp.concatenate([routes[:, 2:], routes[:, :2]], axis=1))
    marked = mine > 0
    until = jnp.asarray(np.triu(np.ones((TOK, TOK), np.float32)), jnp.bfloat16)
    rank = jnp.einsum(
        "bes,st->bet", marked.astype(jnp.bfloat16), until, preferred_element_type=jnp.float32
    )
    rank = jnp.where(marked, rank.astype(jnp.int32) - 1, -1)
    groups = jnp.max(rank, axis=(0, 2)) // SLOT_STEP + 1
    row = np.arange(GROUPS * GROUP_ROWS)
    row_slot = row // GROUP_ROWS * SLOT_STEP + row % SLOT_STEP
    row_block = row % GROUP_ROWS // SLOT_STEP
    same = jnp.asarray(row_block[:, None] == np.arange(2 * TOK)[None, :] // TOK)

    def by_pair(v):
        v = v.reshape(PAIRS, 2, CHIP_EXPERTS, TOK).transpose(0, 2, 1, 3)
        return v.reshape(PAIRS, CHIP_EXPERTS, 1, 2 * TOK)

    chosen = (by_pair(rank) == jnp.asarray(row_slot, jnp.int32)[:, None]) & same
    slot_weight = jnp.sum(jnp.where(chosen, by_pair(mine), 0.0), axis=3)
    slot_weight = slot_weight.reshape(PAIRS, CHIP_EXPERTS, GROUPS, GROUP_ROWS)
    slot_weight = slot_weight.transpose(1, 2, 0, 3).reshape(CHIP_EXPERTS, BLOCKS * SLOTS, 1)
    pick = chosen.astype(jnp.bfloat16).reshape(PAIRS, PAIR_ROWS, 2 * TOK)
    put = pick.reshape(PAIRS, PAIR_ROWS, 2, TOK).transpose(0, 2, 3, 1)
    put = put.reshape(BLOCKS, TOK, PAIR_ROWS)
    return groups, pick, put, slot_weight


def spread(tokens, weights, routes, core):
    held = [tokens[None, :, OFFSET[p] : OFFSET[p] + PART[p]] for p in range(PARTS)]
    weights, far = list(weights), []
    for stage in range(STAGES):
        if stage != 1 and len(far) < len(weights):
            far.append(lax.ppermute(weights[len(far)], AXES, core_pairs()))
        got = [lax.ppermute(held[p], AXES, stage_pairs(p, stage)) for p in range(PARTS)]
        if stage == STAGES - 1:
            return list(zip(held, got)), far, plan
        held = [jnp.concatenate([h, g], axis=0) for h, g in zip(held, got)]
        if stage == 3:
            plan = routing(routes, core)
        if 1 <= stage <= 3:
            held, far, weights, routes = lax.optimization_barrier((held, far, weights, routes))
        if stage == 4:
            held, plan = lax.optimization_barrier((held, plan))


def add(a, b):
    return (a.astype(jnp.float32) + b.astype(jnp.float32)).astype(jnp.bfloat16)


def collect(high, low):
    for stage in reversed(range(STAGES)):
        got = [lax.ppermute(high[p], AXES, stage_pairs(p, stage)) for p in range(PARTS)]
        if stage:
            got, low = lax.optimization_barrier((got, low))
            cut = 1 << (stage - 1)
            high = [add(keep[cut:], came[cut:]) for keep, came in zip(low, got)]
            low = [add(keep[:cut], came[:cut]) for keep, came in zip(low, got)]
    return [keep[0].astype(jnp.float32) + came[0].astype(jnp.float32) for keep, came in zip(low, got)]


def on_device(
    tokens, keep_mask, expert_ids, route_weight, w_gate, w_up, w_down, norm_gain, kv_weight
):
    y, z, c, x = (lax.axis_index(a) for a in AXES)
    me = ((y * 4 + z) * 2 + c) * 4 + x
    place_all, owner_all = place_tables()
    place = lax.dynamic_index_in_dim(jnp.asarray(place_all), me, 0, keepdims=False)
    owner = lax.dynamic_index_in_dim(jnp.asarray(owner_all), me, 0, keepdims=False)

    experts = CHIP_EXPERTS * BLOCKS
    live = (keep_mask > 0)[None, None, :]
    named = expert_ids.T[None] == jnp.arange(experts, dtype=jnp.int32)[:, None, None]
    routes = jnp.sum(jnp.where(named & live, route_weight.T[None], 0.0), axis=1)
    routes = routes.reshape(BLOCKS, CHIP_EXPERTS, TOK)
    routes = lax.all_to_all(routes, ("y", "z"), split_axis=0, concat_axis=0, tiled=True)
    own = (w_gate, w_up, w_down)
    pieces, far, plan = spread(tokens, own, routes, c)
    groups, pick, put, slot_weight = plan

    outs = run_experts(place, owner, groups, pick, put, slot_weight, pieces, own, far)
    ys, high = outs[:PARTS], outs[PARTS:]
    low = [scatter_rows(p, owner, put, ys[p]) for p in range(PARTS)]
    summed = jnp.concatenate(collect(high, low), axis=1)
    mixed_out = (tokens.astype(jnp.float32) + summed).astype(jnp.bfloat16)

    full = [mixed_out] + [lax.ppermute(mixed_out, AXES, x_pairs(m)) for m in (1, 2, 3)]
    full = jnp.concatenate(full, axis=1).astype(jnp.float32)
    order = [jnp.bitwise_xor(x, m) * WIDTH for m in range(4)]
    gain = jnp.concatenate([lax.dynamic_slice_in_dim(norm_gain, o, WIDTH) for o in order])
    kv = jnp.concatenate([lax.dynamic_slice_in_dim(kv_weight, o, WIDTH) for o in order])
    mean_square = jnp.mean(full * full, axis=-1, keepdims=True)
    normed = (full * lax.rsqrt(mean_square + 1e-06) * gain).astype(jnp.bfloat16)
    kv_rows = jnp.dot(normed, kv, preferred_element_type=jnp.float32).astype(jnp.bfloat16)
    return (mixed_out, kv_rows)


def solution(mesh):
    fine = Mesh(mesh.devices.reshape(SIZES), AXES)
    ep = ("y", "z", "c")
    in_specs = (
        P(ep, "x"),
        P(ep),
        P(ep, None),
        P(ep, None),
        P(ep, None, "x"),
        P(ep, None, "x"),
        P(ep, "x", None),
        P(),
        P(None, "x"),
    )
    out_specs = (P(ep, "x"), P(ep, "x"))
    return jax.shard_map(
        on_device, mesh=fine, in_specs=in_specs, out_specs=out_specs, check_vma=False
    )
```

```python
import functools

import jax
import jax.numpy as jnp
import numpy as np
from jax import lax
from jax.experimental import pallas as pl
from jax.experimental.pallas import tpu as pltpu
from jax.sharding import Mesh, PartitionSpec as P

AXES = ("y", "z", "c", "x")
SIZES = (4, 4, 2, 4)
LINKS = (("x", 1), ("y", 3), ("z", 1), ("x", 3), ("y", 1), ("z", 3))
STAGES = len(LINKS)
PEERS = 1 << STAGES
HALF = PEERS // 2
BLOCKS = 16
TOK = 128
WIDTH = 1024
SLOTS = 32
CHIP_EXPERTS = 4
PART = (384, 384, 256)
OFFSET = (0, 384, 768)
PARTS = len(PART)
PAIRS = BLOCKS // 2
GROUPS = 4
SLOT_STEP = SLOTS // GROUPS
GROUP_ROWS = 2 * SLOT_STEP
TILE = PAIRS * GROUP_ROWS
PAIR_ROWS = CHIP_EXPERTS * GROUPS * GROUP_ROWS


def link_of(part, core, stage):
    return LINKS[(2 * part + core + stage) % STAGES]


def device_number(at):
    return ((at["y"] * 4 + at["z"]) * 2 + at["c"]) * 4 + at["x"]


def all_places():
    for y in range(4):
        for z in range(4):
            for c in range(2):
                for x in range(4):
                    yield dict(y=y, z=z, c=c, x=x)


def stage_pairs(part, stage):
    pairs = []
    for at in all_places():
        axis, mask = link_of(part, at["c"], stage)
        to = dict(at)
        to[axis] ^= mask
        pairs.append((device_number(at), device_number(to)))
    return pairs


def core_pairs():
    return [(device_number(at), device_number(dict(at, c=1 - at["c"]))) for at in all_places()]


def x_pairs(mask):
    return [(device_number(at), device_number(dict(at, x=at["x"] ^ mask))) for at in all_places()]


def place_table():
    place = np.zeros((128, PARTS, BLOCKS * 4), np.int32)
    for at in all_places():
        for part in range(PARTS):
            for j in range(PEERS):
                to = dict(at)
                for stage in range(STAGES):
                    if j >> stage & 1:
                        axis, mask = link_of(part, at["c"], stage)
                        to[axis] ^= mask
                place[device_number(at), part, (to["y"] * 4 + to["z"]) * 4 + to["x"]] = j
    return place.reshape(128, -1)


def hidden_kernel(
    groups, pick, weight, tokens, g_own, u_own, g_far, u_far, out, rows, tok, wide, tok_sems, weight_sems
):
    ff = g_own.shape[2]

    def weight_copies(e):
        gate, up = (g_own, u_own) if e < 2 else (g_far, u_far)
        slot, at = e % 2, e % 2
        return (
            pltpu.make_async_copy(gate.at[at], wide.at[slot, :, pl.ds(0, ff)], weight_sems.at[slot, 0]),
            pltpu.make_async_copy(up.at[at], wide.at[slot, :, pl.ds(ff, ff)], weight_sems.at[slot, 1]),
        )

    def token_copies(pair, slot):
        return [
            pltpu.make_async_copy(
                tokens.at[(2 * pair + blk) * 4 + x],
                tok.at[slot, pl.ds(blk * TOK, TOK), pl.ds(x * WIDTH, WIDTH)],
                tok_sems.at[slot, blk * 4 + x],
            )
            for blk in range(2)
            for x in range(4)
        ]

    for copy in token_copies(0, 0) + list(weight_copies(0)):
        copy.start()

    @pl.loop(0, PAIRS)
    def _(pair):
        slot = lax.rem(pair, 2)

        @pl.when(pair + 1 < PAIRS)
        def _():
            for copy in token_copies(pair + 1, 1 - slot):
                copy.start()

        for copy in token_copies(pair, slot):
            copy.wait()
        at = pl.multiple_of(pair * GROUP_ROWS, GROUP_ROWS)
        for x in range(4):
            cols = slice(x * WIDTH, (x + 1) * WIDTH)
            picked = jnp.dot(pick[pair], tok[slot, :, cols], preferred_element_type=jnp.float32)
            picked = picked.astype(jnp.bfloat16)
            for e in range(CHIP_EXPERTS):
                for g in range(GROUPS):
                    first = (e * GROUPS + g) * GROUP_ROWS
                    rows[e, pl.ds(g * TILE + at, GROUP_ROWS), cols] = picked[first : first + GROUP_ROWS]

    for copy in weight_copies(1):
        copy.start()
    for e in range(CHIP_EXPERTS):
        slot = e % 2
        for copy in weight_copies(e):
            copy.wait()

        @pl.loop(0, lax.div(groups[e] + 1, 2))
        def _(g, e=e, slot=slot):
            for i in range(2):
                tile = pl.ds(pl.multiple_of((2 * g + i) * TILE, TILE), TILE)
                both = jnp.dot(rows[e, tile, :], wide[slot], preferred_element_type=jnp.float32)
                product = jax.nn.silu(both[:, :ff]) * both[:, ff:] * weight[e, tile]
                out[e, tile] = product.astype(jnp.bfloat16)

        if e + 2 < CHIP_EXPERTS:
            for copy in weight_copies(e + 2):
                copy.start()


def find_hidden(groups, pick, weight, tokens, own, far):
    ff = own[0].shape[2]
    n = BLOCKS * SLOTS
    anywhere = pl.BlockSpec(memory_space=pl.ANY)
    vmem = pl.BlockSpec(memory_space=pltpu.VMEM)
    smem = pl.BlockSpec(memory_space=pltpu.SMEM)
    return pl.pallas_call(
        hidden_kernel,
        in_specs=[smem, vmem, vmem] + [anywhere] * 5,
        out_specs=vmem,
        out_shape=jax.ShapeDtypeStruct((CHIP_EXPERTS, n, ff), jnp.bfloat16),
        scratch_shapes=[
            pltpu.VMEM((CHIP_EXPERTS, n, 4 * WIDTH), jnp.bfloat16),
            pltpu.VMEM((2, 2 * TOK, 4 * WIDTH), jnp.bfloat16),
            pltpu.VMEM((2, 4 * WIDTH, 2 * ff), jnp.bfloat16),
            pltpu.SemaphoreType.DMA((2, 8)),
            pltpu.SemaphoreType.DMA((2, 2)),
        ],
        compiler_params=pltpu.CompilerParams(vmem_limit_bytes=48 << 20),
        cost_estimate=pl.CostEstimate(
            flops=2 * 2048 * 4096 * 1024, bytes_accessed=100 << 20, transcendentals=2048 * 384
        ),
        name="hidden",
    )(groups, pick, weight, tokens, *own, *far)


def down_kernel(
    part, groups, place, put, hidden, d_own, d_far, low, high, weights, y, sums, weight_sems, sum_sems
):
    f = PART[part]

    def weight_copies(e):
        return [
            pltpu.make_async_copy(
                (d_own if e < 2 else d_far).at[e % 2, :, pl.ds(x * WIDTH + OFFSET[part], f)],
                weights.at[e, :, pl.ds(x * f, f)],
                weight_sems.at[e, x],
            )
            for x in range(4)
        ]

    for e in range(CHIP_EXPERTS):
        for copy in weight_copies(e):
            copy.start()
    for e in range(CHIP_EXPERTS):
        for copy in weight_copies(e):
            copy.wait()
        for half in range(2):
            tiles = [slice((2 * half + i) * TILE, (2 * half + i + 1) * TILE) for i in range(2)]
            used = groups[e] > 2 * half

            @pl.when(used)
            def _(e=e, tiles=tiles):
                for tile in tiles:
                    for x in range(4):
                        cols = slice(x * f, (x + 1) * f)
                        value = jnp.dot(
                            hidden[e, tile], weights[e, :, cols], preferred_element_type=jnp.float32
                        )
                        y[e, tile, cols] = value.astype(jnp.bfloat16)

            @pl.when(jnp.logical_not(used))
            def _(e=e, tiles=tiles):
                for tile in tiles:
                    y[e, tile] = jnp.zeros((TILE, 4 * f), jnp.bfloat16)

    def leave(pair, slot, start):
        for x in range(4):
            for blk in range(2):
                piece = sums.at[slot, x, pl.ds(blk * TOK, TOK)]
                sem = sum_sems.at[slot, 2 * x + blk]
                if not start:
                    pltpu.make_async_copy(piece, low.at[0], sem).wait()
                    continue
                j = place[part * PEERS + (2 * pair + blk) * 4 + x]

                @pl.when(j < HALF)
                def _(j=j, piece=piece, sem=sem):
                    pltpu.make_async_copy(piece, low.at[j], sem).start()

                @pl.when(j >= HALF)
                def _(j=j, piece=piece, sem=sem):
                    pltpu.make_async_copy(piece, high.at[j - HALF], sem).start()

    @pl.loop(0, PAIRS)
    def _(pair):
        slot = lax.rem(pair, 2)

        @pl.when(pair >= 2)
        def _():
            leave(pair - 2, slot, False)

        at = pl.multiple_of(pair * GROUP_ROWS, GROUP_ROWS)
        for x in range(4):
            terms = [
                y[e, pl.ds(g * TILE + at, GROUP_ROWS), x * f : (x + 1) * f]
                for e in range(CHIP_EXPERTS)
                for g in range(GROUPS)
            ]
            terms = jnp.concatenate(terms, axis=0)
            total = jnp.dot(put[pair], terms, preferred_element_type=jnp.float32)
            sums[slot, x] = total.astype(jnp.bfloat16)
        leave(pair, slot, True)

    for pair in (PAIRS - 2, PAIRS - 1):
        leave(pair, pair % 2, False)


def find_sums(part, groups, place, put, hidden, own, far):
    f, ff = PART[part], own.shape[1]
    n = BLOCKS * SLOTS
    anywhere = pl.BlockSpec(memory_space=pl.ANY)
    vmem = pl.BlockSpec(memory_space=pltpu.VMEM)
    smem = pl.BlockSpec(memory_space=pltpu.SMEM)
    return pl.pallas_call(
        functools.partial(down_kernel, part),
        in_specs=[smem, smem, vmem, vmem, anywhere, anywhere],
        out_specs=[anywhere] * 2,
        out_shape=[jax.ShapeDtypeStruct((HALF, TOK, f), jnp.bfloat16)] * 2,
        scratch_shapes=[
            pltpu.VMEM((CHIP_EXPERTS, ff, 4 * f), jnp.bfloat16),
            pltpu.VMEM((CHIP_EXPERTS, n, 4 * f), jnp.bfloat16),
            pltpu.VMEM((2, 4, 2 * TOK, f), jnp.bfloat16),
            pltpu.SemaphoreType.DMA((CHIP_EXPERTS, 4)),
            pltpu.SemaphoreType.DMA((2, 8)),
        ],
        compiler_params=pltpu.CompilerParams(vmem_limit_bytes=32 << 20),
        cost_estimate=pl.CostEstimate(
            flops=2 * 2048 * 4 * f * (ff + 256), bytes_accessed=40 << 20, transcendentals=0
        ),
        name="sums",
    )(groups, place, put, hidden, own, far)


def routing(routes, core):
    mine = jnp.where(core == 0, routes, jnp.concatenate([routes[:, 2:], routes[:, :2]], axis=1))
    marked = mine > 0
    until = jnp.asarray(np.triu(np.ones((TOK, TOK), np.float32)), jnp.bfloat16)
    rank = jnp.einsum(
        "bes,st->bet", marked.astype(jnp.bfloat16), until, preferred_element_type=jnp.float32
    )
    rank = jnp.where(marked, rank.astype(jnp.int32) - 1, -1)
    groups = jnp.max(rank, axis=(0, 2)) // SLOT_STEP + 1
    row = np.arange(GROUPS * GROUP_ROWS)
    row_slot = row // GROUP_ROWS * SLOT_STEP + row % SLOT_STEP
    row_block = row % GROUP_ROWS // SLOT_STEP
    same = jnp.asarray(row_block[:, None] == np.arange(2 * TOK)[None, :] // TOK)

    def by_pair(v):
        v = v.reshape(PAIRS, 2, CHIP_EXPERTS, TOK).transpose(0, 2, 1, 3)
        return v.reshape(PAIRS, CHIP_EXPERTS, 1, 2 * TOK)

    chosen = (by_pair(rank) == jnp.asarray(row_slot, jnp.int32)[:, None]) & same
    slot_weight = jnp.sum(jnp.where(chosen, by_pair(mine), 0.0), axis=3)
    slot_weight = slot_weight.reshape(PAIRS, CHIP_EXPERTS, GROUPS, GROUP_ROWS)
    slot_weight = slot_weight.transpose(1, 2, 0, 3).reshape(CHIP_EXPERTS, BLOCKS * SLOTS, 1)
    pick = chosen.astype(jnp.bfloat16).reshape(PAIRS, PAIR_ROWS, 2 * TOK)
    put = pick.transpose(0, 2, 1)
    return groups, pick, put, slot_weight


def add(a, b):
    return (a.astype(jnp.float32) + b.astype(jnp.float32)).astype(jnp.bfloat16)


def collect(high, low, part):
    for stage in reversed(range(STAGES)):
        got = lax.ppermute(high, AXES, stage_pairs(part, stage))
        if stage:
            cut = 1 << (stage - 1)
            high, low = add(low[cut:], got[cut:]), add(low[:cut], got[:cut])
    return low[0].astype(jnp.float32) + got[0].astype(jnp.float32)


def on_device(
    tokens, keep_mask, expert_ids, route_weight, w_gate, w_up, w_down, norm_gain, kv_weight
):
    y, z, c, x = (lax.axis_index(a) for a in AXES)
    me = ((y * 4 + z) * 2 + c) * 4 + x
    place = lax.dynamic_index_in_dim(jnp.asarray(place_table()), me, 0, keepdims=False)

    experts = CHIP_EXPERTS * BLOCKS
    live = (keep_mask > 0)[None, None, :]
    named = expert_ids.T[None] == jnp.arange(experts, dtype=jnp.int32)[:, None, None]
    routes = jnp.sum(jnp.where(named & live, route_weight.T[None], 0.0), axis=1)
    routes = routes.reshape(BLOCKS, CHIP_EXPERTS, TOK)
    routes = lax.all_to_all(routes, ("y", "z"), split_axis=0, concat_axis=0, tiled=True)
    everyone = lax.all_gather(tokens, ("y", "z", "x"), axis=0)
    own = (w_gate, w_up, w_down)
    far = [lax.ppermute(w, AXES, core_pairs()) for w in own]
    groups, pick, put, slot_weight = routing(routes, c)
    hidden = find_hidden(groups, pick, slot_weight, everyone, own[:2], far[:2])
    sums = [find_sums(p, groups, place, put, hidden, own[2], far[2]) for p in range(PARTS)]
    summed = jnp.concatenate([collect(high, low, p) for p, (low, high) in enumerate(sums)], axis=1)
    mixed_out = (tokens.astype(jnp.float32) + summed).astype(jnp.bfloat16)

    full = [mixed_out] + [lax.ppermute(mixed_out, AXES, x_pairs(m)) for m in (1, 2, 3)]
    full = jnp.concatenate(full, axis=1).astype(jnp.float32)
    order = [jnp.bitwise_xor(x, m) * WIDTH for m in range(4)]
    gain = jnp.concatenate([lax.dynamic_slice_in_dim(norm_gain, o, WIDTH) for o in order])
    kv = jnp.concatenate([lax.dynamic_slice_in_dim(kv_weight, o, WIDTH) for o in order])
    mean_square = jnp.mean(full * full, axis=-1, keepdims=True)
    normed = (full * lax.rsqrt(mean_square + 1e-06) * gain).astype(jnp.bfloat16)
    kv_rows = jnp.dot(normed, kv, preferred_element_type=jnp.float32).astype(jnp.bfloat16)
    return (mixed_out, kv_rows)


def solution(mesh):
    fine = Mesh(mesh.devices.reshape(SIZES), AXES)
    ep = ("y", "z", "c")
    in_specs = (
        P(ep, "x"),
        P(ep),
        P(ep, None),
        P(ep, None),
        P(ep, None, "x"),
        P(ep, None, "x"),
        P(ep, "x", None),
        P(),
        P(None, "x"),
    )
    out_specs = (P(ep, "x"), P(ep, "x"))
    return jax.shard_map(
        on_device, mesh=fine, in_specs=in_specs, out_specs=out_specs, check_vma=False
    )
```

```python
import functools

import jax
import jax.numpy as jnp
import numpy as np
from jax import lax
from jax.experimental import pallas as pl
from jax.experimental.pallas import tpu as pltpu
from jax.sharding import Mesh, PartitionSpec as P

AXES = ("y", "z", "c", "x")
SIZES = (4, 4, 2, 4)
LINKS = (("x", 1), ("y", 3), ("z", 1), ("x", 3), ("y", 1), ("z", 3))
STAGES = len(LINKS)
PEERS = 1 << STAGES
HALF = PEERS // 2
BLOCKS = 16
TOK = 128
WIDTH = 1024
SLOTS = 32
CHIP_EXPERTS = 4
LANES = 128
TILES = WIDTH // LANES
ROWS = (352, 336, 336)
ROW_AT = (0, 352, 688)
PARTS = len(ROWS)
PAIRS = BLOCKS // 2
GROUPS = 4
SLOT_STEP = SLOTS // GROUPS
GROUP_ROWS = 2 * SLOT_STEP
TILE = PAIRS * GROUP_ROWS
PAIR_ROWS = CHIP_EXPERTS * GROUPS * GROUP_ROWS


def tiles_of(part):
    first, last = ROW_AT[part], ROW_AT[part] + ROWS[part]
    found = []
    for tile in range(first // TOK, -(-last // TOK)):
        start, stop = max(first - tile * TOK, 0), min(last - tile * TOK, TOK)
        found.append((tile, start, stop, tile * TOK + start - first))
    return found


def link_of(part, core, stage):
    return LINKS[(2 * part + core + stage) % STAGES]


def device_number(at):
    return ((at["y"] * 4 + at["z"]) * 2 + at["c"]) * 4 + at["x"]


def all_places():
    for y in range(4):
        for z in range(4):
            for c in range(2):
                for x in range(4):
                    yield dict(y=y, z=z, c=c, x=x)


def stage_pairs(part, stage):
    pairs = []
    for at in all_places():
        axis, mask = link_of(part, at["c"], stage)
        to = dict(at)
        to[axis] ^= mask
        pairs.append((device_number(at), device_number(to)))
    return pairs


def core_pairs():
    return [(device_number(at), device_number(dict(at, c=1 - at["c"]))) for at in all_places()]


def x_pairs(mask):
    return [(device_number(at), device_number(dict(at, x=at["x"] ^ mask))) for at in all_places()]


def place_table():
    place = np.zeros((128, PARTS, BLOCKS * 4), np.int32)
    for at in all_places():
        for part in range(PARTS):
            for j in range(PEERS):
                to = dict(at)
                for stage in range(STAGES):
                    if j >> stage & 1:
                        axis, mask = link_of(part, at["c"], stage)
                        to[axis] ^= mask
                place[device_number(at), part, (to["y"] * 4 + to["z"]) * 4 + to["x"]] = j
    return place.reshape(128, -1)


def hidden_kernel(
    place, groups, pick, weight, lo0, hi0, lo1, hi1, lo2, hi2, g_own, u_own, g_far, u_far,
    out, rows, tok, wide, tok_sems, weight_sems,
):
    low, high = (lo0, lo1, lo2), (hi0, hi1, hi2)
    ff = g_own.shape[2]

    def weight_copies(e):
        gate, up = (g_own, u_own) if e < 2 else (g_far, u_far)
        slot, at = e % 2, e % 2
        return (
            pltpu.make_async_copy(gate.at[at], wide.at[slot, :, pl.ds(0, ff)], weight_sems.at[slot, 0]),
            pltpu.make_async_copy(up.at[at], wide.at[slot, :, pl.ds(ff, ff)], weight_sems.at[slot, 1]),
        )

    def fetch(pair, slot, start):
        for blk in range(2):
            for x in range(4):
                for part in range(PARTS):
                    to = tok.at[slot, blk, x, pl.ds(ROW_AT[part], ROWS[part])]
                    sem = tok_sems.at[slot, (blk * 4 + x) * PARTS + part]
                    if not start:
                        pltpu.make_async_copy(low[part].at[0], to, sem).wait()
                        continue
                    j = place[part * PEERS + (2 * pair + blk) * 4 + x]

                    @pl.when(j < HALF)
                    def _(part=part, j=j, to=to, sem=sem):
                        pltpu.make_async_copy(low[part].at[j], to, sem).start()

                    @pl.when(j >= HALF)
                    def _(part=part, j=j, to=to, sem=sem):
                        pltpu.make_async_copy(high[part].at[j - HALF], to, sem).start()

    fetch(0, 0, True)
    for copy in weight_copies(0):
        copy.start()

    @pl.loop(0, PAIRS)
    def _(pair):
        slot = lax.rem(pair, 2)

        @pl.when(pair + 1 < PAIRS)
        def _():
            fetch(pair + 1, 1 - slot, True)

        fetch(pair, slot, False)
        at = pl.multiple_of(pair * GROUP_ROWS, GROUP_ROWS)
        for x in range(4):
            cols = slice(x * WIDTH, (x + 1) * WIDTH)
            held = [
                jnp.concatenate([tok[slot, blk, x, t * TOK : (t + 1) * TOK] for blk in range(2)], axis=0)
                for t in range(TILES)
            ]
            held = jnp.concatenate(held, axis=1)
            picked = jnp.dot(pick[pair], held, preferred_element_type=jnp.float32)
            picked = picked.astype(jnp.bfloat16)
            for e in range(CHIP_EXPERTS):
                for g in range(GROUPS):
                    first = (e * GROUPS + g) * GROUP_ROWS
                    rows[e, pl.ds(g * TILE + at, GROUP_ROWS), cols] = picked[first : first + GROUP_ROWS]

    for copy in weight_copies(1):
        copy.start()
    for e in range(CHIP_EXPERTS):
        slot = e % 2
        for copy in weight_copies(e):
            copy.wait()

        @pl.loop(0, lax.div(groups[e] + 1, 2))
        def _(g, e=e, slot=slot):
            for i in range(2):
                tile = pl.ds(pl.multiple_of((2 * g + i) * TILE, TILE), TILE)
                both = jnp.dot(rows[e, tile, :], wide[slot], preferred_element_type=jnp.float32)
                product = jax.nn.silu(both[:, :ff]) * both[:, ff:] * weight[e, tile]
                out[e, tile] = product.astype(jnp.bfloat16)

        if e + 2 < CHIP_EXPERTS:
            for copy in weight_copies(e + 2):
                copy.start()


def find_hidden(place, groups, pick, weight, pieces, own, far):
    flat = [half for pair in pieces for half in pair]
    ff = own[0].shape[2]
    n = BLOCKS * SLOTS
    anywhere = pl.BlockSpec(memory_space=pl.ANY)
    vmem = pl.BlockSpec(memory_space=pltpu.VMEM)
    smem = pl.BlockSpec(memory_space=pltpu.SMEM)
    return pl.pallas_call(
        hidden_kernel,
        in_specs=[smem, smem, vmem, vmem] + [anywhere] * 10,
        out_specs=vmem,
        out_shape=jax.ShapeDtypeStruct((CHIP_EXPERTS, n, ff), jnp.bfloat16),
        scratch_shapes=[
            pltpu.VMEM((CHIP_EXPERTS, n, 4 * WIDTH), jnp.bfloat16),
            pltpu.VMEM((2, 2, 4, TILES * TOK, LANES), jnp.bfloat16),
            pltpu.VMEM((2, 4 * WIDTH, 2 * ff), jnp.bfloat16),
            pltpu.SemaphoreType.DMA((2, 8 * PARTS)),
            pltpu.SemaphoreType.DMA((2, 2)),
        ],
        compiler_params=pltpu.CompilerParams(vmem_limit_bytes=48 << 20),
        cost_estimate=pl.CostEstimate(
            flops=2 * 2048 * 4096 * 1024, bytes_accessed=100 << 20, transcendentals=2048 * 384
        ),
        name="hidden",
    )(place, groups, pick, weight, *flat, *own, *far)


def down_kernel(
    part, groups, place, put, hidden, d_own, d_far, low, high, weights, y, sums, weight_sems, sum_sems
):
    tiles_in = tiles_of(part)
    f, begin = len(tiles_in) * LANES, tiles_in[0][0] * LANES

    def weight_copies(e):
        return [
            pltpu.make_async_copy(
                (d_own if e < 2 else d_far).at[e % 2, :, pl.ds(x * WIDTH + begin, f)],
                weights.at[e, :, pl.ds(x * f, f)],
                weight_sems.at[e, x],
            )
            for x in range(4)
        ]

    for e in range(CHIP_EXPERTS):
        for copy in weight_copies(e):
            copy.start()
    for e in range(CHIP_EXPERTS):
        for copy in weight_copies(e):
            copy.wait()
        for half in range(2):
            tiles = [slice((2 * half + i) * TILE, (2 * half + i + 1) * TILE) for i in range(2)]
            used = groups[e] > 2 * half

            @pl.when(used)
            def _(e=e, tiles=tiles):
                for tile in tiles:
                    for x in range(4):
                        cols = slice(x * f, (x + 1) * f)
                        value = jnp.dot(
                            hidden[e, tile], weights[e, :, cols], preferred_element_type=jnp.float32
                        )
                        y[e, tile, cols] = value.astype(jnp.bfloat16)

            @pl.when(jnp.logical_not(used))
            def _(e=e, tiles=tiles):
                for tile in tiles:
                    y[e, tile] = jnp.zeros((TILE, 4 * f), jnp.bfloat16)

    def leave(pair, slot, start):
        for x in range(4):
            for blk in range(2):
                piece = sums.at[slot, x, blk]
                sem = sum_sems.at[slot, 2 * x + blk]
                if not start:
                    pltpu.make_async_copy(piece, low.at[0], sem).wait()
                    continue
                j = place[part * PEERS + (2 * pair + blk) * 4 + x]

                @pl.when(j < HALF)
                def _(j=j, piece=piece, sem=sem):
                    pltpu.make_async_copy(piece, low.at[j], sem).start()

                @pl.when(j >= HALF)
                def _(j=j, piece=piece, sem=sem):
                    pltpu.make_async_copy(piece, high.at[j - HALF], sem).start()

    @pl.loop(0, PAIRS)
    def _(pair):
        slot = lax.rem(pair, 2)

        @pl.when(pair >= 2)
        def _():
            leave(pair - 2, slot, False)

        at = pl.multiple_of(pair * GROUP_ROWS, GROUP_ROWS)
        for x in range(4):
            terms = [
                y[e, pl.ds(g * TILE + at, GROUP_ROWS), x * f : (x + 1) * f]
                for e in range(CHIP_EXPERTS)
                for g in range(GROUPS)
            ]
            terms = jnp.concatenate(terms, axis=0)
            total = jnp.dot(put[pair], terms, preferred_element_type=jnp.float32)
            total = total.astype(jnp.bfloat16)
            for blk in range(2):
                for i, (_, start, stop, to) in enumerate(tiles_in):
                    sums[slot, x, blk, to : to + stop - start] = total[
                        blk * TOK + start : blk * TOK + stop, i * LANES : (i + 1) * LANES
                    ]
        leave(pair, slot, True)

    for pair in (PAIRS - 2, PAIRS - 1):
        leave(pair, pair % 2, False)


def find_sums(part, groups, place, put, hidden, own, far):
    f, ff = len(tiles_of(part)) * LANES, own.shape[1]
    n = BLOCKS * SLOTS
    anywhere = pl.BlockSpec(memory_space=pl.ANY)
    vmem = pl.BlockSpec(memory_space=pltpu.VMEM)
    smem = pl.BlockSpec(memory_space=pltpu.SMEM)
    return pl.pallas_call(
        functools.partial(down_kernel, part),
        in_specs=[smem, smem, vmem, vmem, anywhere, anywhere],
        out_specs=[anywhere] * 2,
        out_shape=[jax.ShapeDtypeStruct((HALF, ROWS[part], LANES), jnp.bfloat16)] * 2,
        scratch_shapes=[
            pltpu.VMEM((CHIP_EXPERTS, ff, 4 * f), jnp.bfloat16),
            pltpu.VMEM((CHIP_EXPERTS, n, 4 * f), jnp.bfloat16),
            pltpu.VMEM((2, 4, 2, ROWS[part], LANES), jnp.bfloat16),
            pltpu.SemaphoreType.DMA((CHIP_EXPERTS, 4)),
            pltpu.SemaphoreType.DMA((2, 8)),
        ],
        compiler_params=pltpu.CompilerParams(vmem_limit_bytes=32 << 20),
        cost_estimate=pl.CostEstimate(
            flops=2 * 2048 * 4 * f * (ff + 256), bytes_accessed=40 << 20, transcendentals=0
        ),
        name="sums",
    )(groups, place, put, hidden, own, far)


def routing(routes, core):
    mine = jnp.where(core == 0, routes, jnp.concatenate([routes[:, 2:], routes[:, :2]], axis=1))
    marked = mine > 0
    until = jnp.asarray(np.triu(np.ones((TOK, TOK), np.float32)), jnp.bfloat16)
    rank = jnp.einsum(
        "bes,st->bet", marked.astype(jnp.bfloat16), until, preferred_element_type=jnp.float32
    )
    rank = jnp.where(marked, rank.astype(jnp.int32) - 1, -1)
    groups = jnp.max(rank, axis=(0, 2)) // SLOT_STEP + 1
    row = np.arange(GROUPS * GROUP_ROWS)
    row_slot = row // GROUP_ROWS * SLOT_STEP + row % SLOT_STEP
    row_block = row % GROUP_ROWS // SLOT_STEP
    same = jnp.asarray(row_block[:, None] == np.arange(2 * TOK)[None, :] // TOK)

    def by_pair(v):
        v = v.reshape(PAIRS, 2, CHIP_EXPERTS, TOK).transpose(0, 2, 1, 3)
        return v.reshape(PAIRS, CHIP_EXPERTS, 1, 2 * TOK)

    chosen = (by_pair(rank) == jnp.asarray(row_slot, jnp.int32)[:, None]) & same
    slot_weight = jnp.sum(jnp.where(chosen, by_pair(mine), 0.0), axis=3)
    slot_weight = slot_weight.reshape(PAIRS, CHIP_EXPERTS, GROUPS, GROUP_ROWS)
    slot_weight = slot_weight.transpose(1, 2, 0, 3).reshape(CHIP_EXPERTS, BLOCKS * SLOTS, 1)
    pick = chosen.astype(jnp.bfloat16).reshape(PAIRS, PAIR_ROWS, 2 * TOK)
    put = pick.transpose(0, 2, 1)
    return groups, pick, put, slot_weight


def spread(tokens, weights, routes):
    tiled = tokens.reshape(TOK, TILES, LANES).transpose(1, 0, 2).reshape(TILES * TOK, LANES)
    held = [tiled[None, ROW_AT[p] : ROW_AT[p] + ROWS[p]] for p in range(PARTS)]
    weights, far = list(weights), []
    for stage in range(STAGES):
        if stage != 1 and len(far) < len(weights):
            far.append(lax.ppermute(weights[len(far)], AXES, core_pairs()))
        got = [lax.ppermute(held[p], AXES, stage_pairs(p, stage)) for p in range(PARTS)]
        if stage == STAGES - 1:
            return list(zip(held, got)), far, routes
        held = [jnp.concatenate([h, g], axis=0) for h, g in zip(held, got)]
        if 1 <= stage <= 2:
            held, far, weights = lax.optimization_barrier((held, far, weights))
        if stage == 3:
            held, far, routes = lax.optimization_barrier((held, far, routes))


def add(a, b):
    return (a.astype(jnp.float32) + b.astype(jnp.float32)).astype(jnp.bfloat16)


def collect(high, low, part):
    for stage in reversed(range(STAGES)):
        got = lax.ppermute(high, AXES, stage_pairs(part, stage))
        if stage:
            cut = 1 << (stage - 1)
            high, low = add(low[cut:], got[cut:]), add(low[:cut], got[:cut])
    return low[0].astype(jnp.float32) + got[0].astype(jnp.float32)


def on_device(
    tokens, keep_mask, expert_ids, route_weight, w_gate, w_up, w_down, norm_gain, kv_weight
):
    y, z, c, x = (lax.axis_index(a) for a in AXES)
    me = ((y * 4 + z) * 2 + c) * 4 + x
    place = lax.dynamic_index_in_dim(jnp.asarray(place_table()), me, 0, keepdims=False)

    experts = CHIP_EXPERTS * BLOCKS
    live = (keep_mask > 0)[None, None, :]
    named = expert_ids.T[None] == jnp.arange(experts, dtype=jnp.int32)[:, None, None]
    routes = jnp.sum(jnp.where(named & live, route_weight.T[None], 0.0), axis=1)
    routes = routes.reshape(BLOCKS, CHIP_EXPERTS, TOK)
    routes = lax.all_to_all(routes, ("y", "z"), split_axis=0, concat_axis=0, tiled=True)
    own = (w_gate, w_up, w_down)
    pieces, far, routes = spread(tokens, own, routes)
    groups, pick, put, slot_weight = routing(routes, c)
    hidden = find_hidden(place, groups, pick, slot_weight, pieces, own[:2], far[:2])
    totals = []
    for part in range(PARTS):
        low, high = find_sums(part, groups, place, put, hidden, own[2], far[2])
        hidden, low, high = lax.optimization_barrier((hidden, low, high))
        totals.append((high, low))
    summed = jnp.concatenate([collect(*totals[p], p) for p in range(PARTS)], axis=0)
    summed = summed.reshape(TILES, TOK, LANES).transpose(1, 0, 2).reshape(TOK, WIDTH)
    mixed_out = (tokens.astype(jnp.float32) + summed).astype(jnp.bfloat16)

    full = [mixed_out] + [lax.ppermute(mixed_out, AXES, x_pairs(m)) for m in (1, 2, 3)]
    full = jnp.concatenate(full, axis=1).astype(jnp.float32)
    order = [jnp.bitwise_xor(x, m) * WIDTH for m in range(4)]
    gain = jnp.concatenate([lax.dynamic_slice_in_dim(norm_gain, o, WIDTH) for o in order])
    kv = jnp.concatenate([lax.dynamic_slice_in_dim(kv_weight, o, WIDTH) for o in order])
    mean_square = jnp.mean(full * full, axis=-1, keepdims=True)
    normed = (full * lax.rsqrt(mean_square + 1e-06) * gain).astype(jnp.bfloat16)
    kv_rows = jnp.dot(normed, kv, preferred_element_type=jnp.float32).astype(jnp.bfloat16)
    return (mixed_out, kv_rows)


def solution(mesh):
    fine = Mesh(mesh.devices.reshape(SIZES), AXES)
    ep = ("y", "z", "c")
    in_specs = (
        P(ep, "x"),
        P(ep),
        P(ep, None),
        P(ep, None),
        P(ep, None, "x"),
        P(ep, None, "x"),
        P(ep, "x", None),
        P(),
        P(None, "x"),
    )
    out_specs = (P(ep, "x"), P(ep, "x"))
    return jax.shard_map(
        on_device, mesh=fine, in_specs=in_specs, out_specs=out_specs, check_vma=False
    )
```

```python
import functools

import jax
import jax.numpy as jnp
import numpy as np
from jax import lax
from jax.experimental import pallas as pl
from jax.experimental.pallas import tpu as pltpu
from jax.sharding import Mesh, PartitionSpec as P

AXES = ("y", "z", "c", "x")
SIZES = (4, 4, 2, 4)
LINKS = (("x", 1), ("y", 3), ("z", 1), ("x", 3), ("y", 1), ("z", 3))
STAGES = len(LINKS)
PEERS = 1 << STAGES
HALF = PEERS // 2
BLOCKS = 16
TOK = 128
WIDTH = 1024
SLOTS = 32
CHIP_EXPERTS = 4
LANES = 128
TILES = WIDTH // LANES
ROWS = (352, 336, 336)
ROW_AT = (0, 352, 688)
PARTS = len(ROWS)
PAIRS = BLOCKS // 2
GROUPS = 4
SLOT_STEP = SLOTS // GROUPS
GROUP_ROWS = 2 * SLOT_STEP
TILE = PAIRS * GROUP_ROWS
PAIR_ROWS = CHIP_EXPERTS * GROUPS * GROUP_ROWS


def tiles_of(part):
    first, last = ROW_AT[part], ROW_AT[part] + ROWS[part]
    found = []
    for tile in range(first // TOK, -(-last // TOK)):
        start, stop = max(first - tile * TOK, 0), min(last - tile * TOK, TOK)
        found.append((tile, start, stop, tile * TOK + start - first))
    return found


def link_of(part, core, stage):
    return LINKS[(2 * part + core + stage) % STAGES]


def device_number(at):
    return ((at["y"] * 4 + at["z"]) * 2 + at["c"]) * 4 + at["x"]


def all_places():
    for y in range(4):
        for z in range(4):
            for c in range(2):
                for x in range(4):
                    yield dict(y=y, z=z, c=c, x=x)


def stage_pairs(part, stage):
    pairs = []
    for at in all_places():
        axis, mask = link_of(part, at["c"], stage)
        to = dict(at)
        to[axis] ^= mask
        pairs.append((device_number(at), device_number(to)))
    return pairs


def core_pairs():
    return [(device_number(at), device_number(dict(at, c=1 - at["c"]))) for at in all_places()]


def x_pairs(mask):
    return [(device_number(at), device_number(dict(at, x=at["x"] ^ mask))) for at in all_places()]


def place_table():
    place = np.zeros((128, PARTS, BLOCKS * 4), np.int32)
    for at in all_places():
        for part in range(PARTS):
            for j in range(PEERS):
                to = dict(at)
                for stage in range(STAGES):
                    if j >> stage & 1:
                        axis, mask = link_of(part, at["c"], stage)
                        to[axis] ^= mask
                place[device_number(at), part, (to["y"] * 4 + to["z"]) * 4 + to["x"]] = j
    return place.reshape(128, -1)


def hidden_kernel(
    place, groups, pick, weight, lo0, hi0, lo1, hi1, lo2, hi2, g_own, u_own, g_far, u_far,
    out, rows, tok, wide, tok_sems, weight_sems,
):
    low, high = (lo0, lo1, lo2), (hi0, hi1, hi2)
    ff = g_own.shape[2]

    def weight_copies(e):
        gate, up = (g_own, u_own) if e < 2 else (g_far, u_far)
        slot, at = e % 2, e % 2
        return (
            pltpu.make_async_copy(gate.at[at], wide.at[slot, :, pl.ds(0, ff)], weight_sems.at[slot, 0]),
            pltpu.make_async_copy(up.at[at], wide.at[slot, :, pl.ds(ff, ff)], weight_sems.at[slot, 1]),
        )

    def fetch(pair, slot, start):
        for blk in range(2):
            for x in range(4):
                for part in range(PARTS):
                    to = tok.at[slot, blk, x, pl.ds(ROW_AT[part], ROWS[part])]
                    sem = tok_sems.at[slot, (blk * 4 + x) * PARTS + part]
                    if not start:
                        pltpu.make_async_copy(low[part].at[0], to, sem).wait()
                        continue
                    j = place[part * PEERS + (2 * pair + blk) * 4 + x]

                    @pl.when(j < HALF)
                    def _(part=part, j=j, to=to, sem=sem):
                        pltpu.make_async_copy(low[part].at[j], to, sem).start()

                    @pl.when(j >= HALF)
                    def _(part=part, j=j, to=to, sem=sem):
                        pltpu.make_async_copy(high[part].at[j - HALF], to, sem).start()

    fetch(0, 0, True)
    for copy in weight_copies(0):
        copy.start()

    @pl.loop(0, PAIRS)
    def _(pair):
        slot = lax.rem(pair, 2)

        @pl.when(pair + 1 < PAIRS)
        def _():
            fetch(pair + 1, 1 - slot, True)

        fetch(pair, slot, False)
        at = pl.multiple_of(pair * GROUP_ROWS, GROUP_ROWS)
        for x in range(4):
            cols = slice(x * WIDTH, (x + 1) * WIDTH)
            held = [
                jnp.concatenate([tok[slot, blk, x, t * TOK : (t + 1) * TOK] for blk in range(2)], axis=0)
                for t in range(TILES)
            ]
            held = jnp.concatenate(held, axis=1)
            picked = jnp.dot(pick[pair], held, preferred_element_type=jnp.float32)
            picked = picked.astype(jnp.bfloat16)
            for e in range(CHIP_EXPERTS):
                for g in range(GROUPS):
                    first = (e * GROUPS + g) * GROUP_ROWS
                    rows[e, pl.ds(g * TILE + at, GROUP_ROWS), cols] = picked[first : first + GROUP_ROWS]

    for copy in weight_copies(1):
        copy.start()
    for e in range(CHIP_EXPERTS):
        slot = e % 2
        for copy in weight_copies(e):
            copy.wait()

        @pl.loop(0, lax.div(groups[e] + 1, 2))
        def _(g, e=e, slot=slot):
            for i in range(2):
                tile = pl.ds(pl.multiple_of((2 * g + i) * TILE, TILE), TILE)
                both = jnp.dot(rows[e, tile, :], wide[slot], preferred_element_type=jnp.float32)
                product = jax.nn.silu(both[:, :ff]) * both[:, ff:] * weight[e, tile]
                out[e, tile] = product.astype(jnp.bfloat16)

        if e + 2 < CHIP_EXPERTS:
            for copy in weight_copies(e + 2):
                copy.start()


def find_hidden(place, groups, pick, weight, pieces, own, far):
    flat = [half for pair in pieces for half in pair]
    ff = own[0].shape[2]
    n = BLOCKS * SLOTS
    anywhere = pl.BlockSpec(memory_space=pl.ANY)
    vmem = pl.BlockSpec(memory_space=pltpu.VMEM)
    smem = pl.BlockSpec(memory_space=pltpu.SMEM)
    return pl.pallas_call(
        hidden_kernel,
        in_specs=[smem, smem, vmem, vmem] + [anywhere] * 10,
        out_specs=vmem,
        out_shape=jax.ShapeDtypeStruct((CHIP_EXPERTS, n, ff), jnp.bfloat16),
        scratch_shapes=[
            pltpu.VMEM((CHIP_EXPERTS, n, 4 * WIDTH), jnp.bfloat16),
            pltpu.VMEM((2, 2, 4, TILES * TOK, LANES), jnp.bfloat16),
            pltpu.VMEM((2, 4 * WIDTH, 2 * ff), jnp.bfloat16),
            pltpu.SemaphoreType.DMA((2, 8 * PARTS)),
            pltpu.SemaphoreType.DMA((2, 2)),
        ],
        compiler_params=pltpu.CompilerParams(vmem_limit_bytes=48 << 20),
        cost_estimate=pl.CostEstimate(
            flops=2 * 2048 * 4096 * 1024, bytes_accessed=100 << 20, transcendentals=2048 * 384
        ),
        name="hidden",
    )(place, groups, pick, weight, *flat, *own, *far)


def down_kernel(
    part, groups, place, put, hidden, d_own, d_far, low, high, weights, y, weight_sems
):
    tiles_in = tiles_of(part)
    f, begin = len(tiles_in) * LANES, tiles_in[0][0] * LANES

    def weight_copies(e):
        return [
            pltpu.make_async_copy(
                (d_own if e < 2 else d_far).at[e % 2, :, pl.ds(x * WIDTH + begin, f)],
                weights.at[e, :, pl.ds(x * f, f)],
                weight_sems.at[e, x],
            )
            for x in range(4)
        ]

    for e in range(CHIP_EXPERTS):
        for copy in weight_copies(e):
            copy.start()
    for e in range(CHIP_EXPERTS):
        for copy in weight_copies(e):
            copy.wait()
        for half in range(2):
            tiles = [slice((2 * half + i) * TILE, (2 * half + i + 1) * TILE) for i in range(2)]
            used = groups[e] > 2 * half

            @pl.when(used)
            def _(e=e, tiles=tiles):
                for tile in tiles:
                    for x in range(4):
                        cols = slice(x * f, (x + 1) * f)
                        value = jnp.dot(
                            hidden[e, tile], weights[e, :, cols], preferred_element_type=jnp.float32
                        )
                        y[e, tile, cols] = value.astype(jnp.bfloat16)

            @pl.when(jnp.logical_not(used))
            def _(e=e, tiles=tiles):
                for tile in tiles:
                    y[e, tile] = jnp.zeros((TILE, 4 * f), jnp.bfloat16)

    @pl.loop(0, PAIRS, unroll=2)
    def _(pair):
        at = pl.multiple_of(pair * GROUP_ROWS, GROUP_ROWS)
        for x in range(4):
            terms = [
                y[e, pl.ds(g * TILE + at, GROUP_ROWS), x * f : (x + 1) * f]
                for e in range(CHIP_EXPERTS)
                for g in range(GROUPS)
            ]
            terms = jnp.concatenate(terms, axis=0)
            total = jnp.dot(put[pair], terms, preferred_element_type=jnp.float32)
            total = total.astype(jnp.bfloat16)
            for blk in range(2):
                piece = [
                    total[blk * TOK + start : blk * TOK + stop, i * LANES : (i + 1) * LANES]
                    for i, (_, start, stop, _) in enumerate(tiles_in)
                ]
                piece = jnp.concatenate(piece, axis=0)
                j = place[part * PEERS + (2 * pair + blk) * 4 + x]
                low[jnp.minimum(j, HALF)] = piece
                high[jnp.where(j < HALF, HALF, j - HALF)] = piece


def find_sums(part, groups, place, put, hidden, own, far):
    f, ff = len(tiles_of(part)) * LANES, own.shape[1]
    n = BLOCKS * SLOTS
    anywhere = pl.BlockSpec(memory_space=pl.ANY)
    vmem = pl.BlockSpec(memory_space=pltpu.VMEM)
    smem = pl.BlockSpec(memory_space=pltpu.SMEM)
    return pl.pallas_call(
        functools.partial(down_kernel, part),
        in_specs=[smem, smem, vmem, vmem, anywhere, anywhere],
        out_specs=[vmem] * 2,
        out_shape=[jax.ShapeDtypeStruct((HALF + 1, ROWS[part], LANES), jnp.bfloat16)] * 2,
        scratch_shapes=[
            pltpu.VMEM((CHIP_EXPERTS, ff, 4 * f), jnp.bfloat16),
            pltpu.VMEM((CHIP_EXPERTS, n, 4 * f), jnp.bfloat16),
            pltpu.SemaphoreType.DMA((CHIP_EXPERTS, 4)),
        ],
        compiler_params=pltpu.CompilerParams(vmem_limit_bytes=32 << 20),
        cost_estimate=pl.CostEstimate(
            flops=2 * 2048 * 4 * f * (ff + 256), bytes_accessed=4 << 20, transcendentals=0
        ),
        name="sums",
    )(groups, place, put, hidden, own, far)


def routing(routes, core):
    mine = jnp.where(core == 0, routes, jnp.concatenate([routes[:, 2:], routes[:, :2]], axis=1))
    marked = mine > 0
    until = jnp.asarray(np.triu(np.ones((TOK, TOK), np.float32)), jnp.bfloat16)
    rank = jnp.einsum(
        "bes,st->bet", marked.astype(jnp.bfloat16), until, preferred_element_type=jnp.float32
    )
    rank = jnp.where(marked, rank.astype(jnp.int32) - 1, -1)
    groups = jnp.max(rank, axis=(0, 2)) // SLOT_STEP + 1
    row = np.arange(GROUPS * GROUP_ROWS)
    row_slot = row // GROUP_ROWS * SLOT_STEP + row % SLOT_STEP
    row_block = row % GROUP_ROWS // SLOT_STEP
    same = jnp.asarray(row_block[:, None] == np.arange(2 * TOK)[None, :] // TOK)

    def by_pair(v):
        v = v.reshape(PAIRS, 2, CHIP_EXPERTS, TOK).transpose(0, 2, 1, 3)
        return v.reshape(PAIRS, CHIP_EXPERTS, 1, 2 * TOK)

    chosen = (by_pair(rank) == jnp.asarray(row_slot, jnp.int32)[:, None]) & same
    slot_weight = jnp.sum(jnp.where(chosen, by_pair(mine), 0.0), axis=3)
    slot_weight = slot_weight.reshape(PAIRS, CHIP_EXPERTS, GROUPS, GROUP_ROWS)
    slot_weight = slot_weight.transpose(1, 2, 0, 3).reshape(CHIP_EXPERTS, BLOCKS * SLOTS, 1)
    pick = chosen.astype(jnp.bfloat16).reshape(PAIRS, PAIR_ROWS, 2 * TOK)
    put = pick.transpose(0, 2, 1)
    return groups, pick, put, slot_weight


def spread(tokens, weights, routes):
    tiled = tokens.reshape(TOK, TILES, LANES).transpose(1, 0, 2).reshape(TILES * TOK, LANES)
    held = [tiled[None, ROW_AT[p] : ROW_AT[p] + ROWS[p]] for p in range(PARTS)]
    weights, far = list(weights), []
    for stage in range(STAGES):
        if stage != 1 and len(far) < len(weights):
            far.append(lax.ppermute(weights[len(far)], AXES, core_pairs()))
        got = [lax.ppermute(held[p], AXES, stage_pairs(p, stage)) for p in range(PARTS)]
        if stage == STAGES - 1:
            return list(zip(held, got)), far, routes
        held = [jnp.concatenate([h, g], axis=0) for h, g in zip(held, got)]
        if 1 <= stage <= 2:
            held, far, weights = lax.optimization_barrier((held, far, weights))
        if stage == 3:
            held, far, routes = lax.optimization_barrier((held, far, routes))


def add(a, b):
    return (a.astype(jnp.float32) + b.astype(jnp.float32)).astype(jnp.bfloat16)


def collect(high, low, part):
    for stage in reversed(range(STAGES)):
        got = lax.ppermute(high, AXES, stage_pairs(part, stage))
        if stage:
            cut = 1 << (stage - 1)
            high = add(low[cut : 2 * cut], got[cut : 2 * cut])
            low = add(low[:cut], got[:cut])
    return low[0].astype(jnp.float32) + got[0].astype(jnp.float32)


def on_device(
    tokens, keep_mask, expert_ids, route_weight, w_gate, w_up, w_down, norm_gain, kv_weight
):
    y, z, c, x = (lax.axis_index(a) for a in AXES)
    me = ((y * 4 + z) * 2 + c) * 4 + x
    place = lax.dynamic_index_in_dim(jnp.asarray(place_table()), me, 0, keepdims=False)

    experts = CHIP_EXPERTS * BLOCKS
    live = (keep_mask > 0)[None, None, :]
    named = expert_ids.T[None] == jnp.arange(experts, dtype=jnp.int32)[:, None, None]
    routes = jnp.sum(jnp.where(named & live, route_weight.T[None], 0.0), axis=1)
    routes = routes.reshape(BLOCKS, CHIP_EXPERTS, TOK)
    routes = lax.all_to_all(routes, ("y", "z"), split_axis=0, concat_axis=0, tiled=True)
    own = (w_gate, w_up, w_down)
    pieces, far, routes = spread(tokens, own, routes)
    groups, pick, put, slot_weight = routing(routes, c)
    hidden = find_hidden(place, groups, pick, slot_weight, pieces, own[:2], far[:2])
    totals = []
    for part in range(PARTS):
        low, high = find_sums(part, groups, place, put, hidden, own[2], far[2])
        hidden, low, high = lax.optimization_barrier((hidden, low, high))
        totals.append((high, low))
    summed = jnp.concatenate([collect(*totals[p], p) for p in range(PARTS)], axis=0)
    summed = summed.reshape(TILES, TOK, LANES).transpose(1, 0, 2).reshape(TOK, WIDTH)
    mixed_out = (tokens.astype(jnp.float32) + summed).astype(jnp.bfloat16)

    full = [mixed_out] + [lax.ppermute(mixed_out, AXES, x_pairs(m)) for m in (1, 2, 3)]
    full = jnp.concatenate(full, axis=1).astype(jnp.float32)
    order = [jnp.bitwise_xor(x, m) * WIDTH for m in range(4)]
    gain = jnp.concatenate([lax.dynamic_slice_in_dim(norm_gain, o, WIDTH) for o in order])
    kv = jnp.concatenate([lax.dynamic_slice_in_dim(kv_weight, o, WIDTH) for o in order])
    mean_square = jnp.mean(full * full, axis=-1, keepdims=True)
    normed = (full * lax.rsqrt(mean_square + 1e-06) * gain).astype(jnp.bfloat16)
    kv_rows = jnp.dot(normed, kv, preferred_element_type=jnp.float32).astype(jnp.bfloat16)
    return (mixed_out, kv_rows)


def solution(mesh):
    fine = Mesh(mesh.devices.reshape(SIZES), AXES)
    ep = ("y", "z", "c")
    in_specs = (
        P(ep, "x"),
        P(ep),
        P(ep, None),
        P(ep, None),
        P(ep, None, "x"),
        P(ep, None, "x"),
        P(ep, "x", None),
        P(),
        P(None, "x"),
    )
    out_specs = (P(ep, "x"), P(ep, "x"))
    return jax.shard_map(
        on_device, mesh=fine, in_specs=in_specs, out_specs=out_specs, check_vma=False
    )
```

```python
import functools

import jax
import jax.numpy as jnp
import numpy as np
from jax import lax
from jax.experimental import pallas as pl
from jax.experimental.pallas import tpu as pltpu
from jax.sharding import Mesh, PartitionSpec as P

AXES = ("y", "z", "c", "x")
SIZES = (4, 4, 2, 4)
LINKS = (("x", 1), ("y", 3), ("z", 1), ("x", 3), ("y", 1), ("z", 3))
STAGES = len(LINKS)
PEERS = 1 << STAGES
HALF = PEERS // 2
BLOCKS = 16
TOK = 128
WIDTH = 1024
SLOTS = 32
CHIP_EXPERTS = 4
LANES = 128
TILES = WIDTH // LANES
ROWS = (352, 336, 336)
ROW_AT = (0, 352, 688)
PARTS = len(ROWS)
PAIRS = BLOCKS // 2
GROUPS = 4
SLOT_STEP = SLOTS // GROUPS
GROUP_ROWS = 2 * SLOT_STEP
TILE = PAIRS * GROUP_ROWS
PAIR_ROWS = CHIP_EXPERTS * GROUPS * GROUP_ROWS


def tiles_of(part):
    first, last = ROW_AT[part], ROW_AT[part] + ROWS[part]
    found = []
    for tile in range(first // TOK, -(-last // TOK)):
        start, stop = max(first - tile * TOK, 0), min(last - tile * TOK, TOK)
        found.append((tile, start, stop, tile * TOK + start - first))
    return found


def link_of(part, core, stage):
    return LINKS[(2 * part + core + stage) % STAGES]


def device_number(at):
    return ((at["y"] * 4 + at["z"]) * 2 + at["c"]) * 4 + at["x"]


def all_places():
    for y in range(4):
        for z in range(4):
            for c in range(2):
                for x in range(4):
                    yield dict(y=y, z=z, c=c, x=x)


def stage_pairs(part, stage):
    pairs = []
    for at in all_places():
        axis, mask = link_of(part, at["c"], stage)
        to = dict(at)
        to[axis] ^= mask
        pairs.append((device_number(at), device_number(to)))
    return pairs


def core_pairs():
    return [(device_number(at), device_number(dict(at, c=1 - at["c"]))) for at in all_places()]


def x_pairs(mask):
    return [(device_number(at), device_number(dict(at, x=at["x"] ^ mask))) for at in all_places()]


def place_table():
    place = np.zeros((128, PARTS, BLOCKS * 4), np.int32)
    for at in all_places():
        for part in range(PARTS):
            for j in range(PEERS):
                to = dict(at)
                for stage in range(STAGES):
                    if j >> stage & 1:
                        axis, mask = link_of(part, at["c"], stage)
                        to[axis] ^= mask
                place[device_number(at), part, (to["y"] * 4 + to["z"]) * 4 + to["x"]] = j
    return place.reshape(128, -1)


def hidden_kernel(
    place, groups, pick, weight, lo0, hi0, lo1, hi1, lo2, hi2, g_own, u_own, g_far, u_far,
    out, rows, tok, wide, tok_sems, weight_sems,
):
    low, high = (lo0, lo1, lo2), (hi0, hi1, hi2)
    ff = g_own.shape[2]

    def weight_copies(gate, up, at, slot):
        return (
            pltpu.make_async_copy(gate.at[at], wide.at[slot, :, pl.ds(0, ff)], weight_sems.at[slot, 0]),
            pltpu.make_async_copy(up.at[at], wide.at[slot, :, pl.ds(ff, ff)], weight_sems.at[slot, 1]),
        )

    def fetch(pair, slot, start):
        for blk in range(2):
            for x in range(4):
                for part in range(PARTS):
                    to = tok.at[slot, blk, x, pl.ds(ROW_AT[part], ROWS[part])]
                    sem = tok_sems.at[slot, (blk * 4 + x) * PARTS + part]
                    if not start:
                        pltpu.make_async_copy(low[part].at[0], to, sem).wait()
                        continue
                    j = place[part * PEERS + (2 * pair + blk) * 4 + x]

                    @pl.when(j < HALF)
                    def _(part=part, j=j, to=to, sem=sem):
                        pltpu.make_async_copy(low[part].at[j], to, sem).start()

                    @pl.when(j >= HALF)
                    def _(part=part, j=j, to=to, sem=sem):
                        pltpu.make_async_copy(high[part].at[j - HALF], to, sem).start()

    fetch(0, 0, True)
    for copy in weight_copies(g_own, u_own, 0, 0):
        copy.start()

    @pl.loop(0, PAIRS)
    def _(pair):
        slot = lax.rem(pair, 2)

        @pl.when(pair + 1 < PAIRS)
        def _():
            fetch(pair + 1, 1 - slot, True)

        fetch(pair, slot, False)
        at = pl.multiple_of(pair * GROUP_ROWS, GROUP_ROWS)
        for x in range(4):
            cols = slice(x * WIDTH, (x + 1) * WIDTH)
            held = [
                jnp.concatenate([tok[slot, blk, x, t * TOK : (t + 1) * TOK] for blk in range(2)], axis=0)
                for t in range(TILES)
            ]
            held = jnp.concatenate(held, axis=1)
            picked = jnp.dot(pick[pair], held, preferred_element_type=jnp.float32)
            picked = picked.astype(jnp.bfloat16)
            for e in range(CHIP_EXPERTS):
                for g in range(GROUPS):
                    first = (e * GROUPS + g) * GROUP_ROWS
                    rows[e, pl.ds(g * TILE + at, GROUP_ROWS), cols] = picked[first : first + GROUP_ROWS]

    for copy in weight_copies(g_own, u_own, 1, 1):
        copy.start()

    @pl.loop(0, CHIP_EXPERTS)
    def _(e):
        slot = lax.rem(e, 2)
        for copy in weight_copies(g_own, u_own, 0, slot):
            copy.wait()

        @pl.loop(0, lax.div(groups[e] + 1, 2))
        def _(g):
            for i in range(2):
                tile = pl.ds(pl.multiple_of((2 * g + i) * TILE, TILE), TILE)
                both = jnp.dot(rows[e, tile, :], wide[slot], preferred_element_type=jnp.float32)
                product = jax.nn.silu(both[:, :ff]) * both[:, ff:] * weight[e, tile]
                out[e, tile] = product.astype(jnp.bfloat16)

        @pl.when(e < 2)
        def _():
            for copy in weight_copies(g_far, u_far, e, slot):
                copy.start()


def find_hidden(place, groups, pick, weight, pieces, own, far):
    flat = [half for pair in pieces for half in pair]
    ff = own[0].shape[2]
    n = BLOCKS * SLOTS
    anywhere = pl.BlockSpec(memory_space=pl.ANY)
    vmem = pl.BlockSpec(memory_space=pltpu.VMEM)
    smem = pl.BlockSpec(memory_space=pltpu.SMEM)
    return pl.pallas_call(
        hidden_kernel,
        in_specs=[smem, smem, vmem, vmem] + [anywhere] * 10,
        out_specs=vmem,
        out_shape=jax.ShapeDtypeStruct((CHIP_EXPERTS, n, ff), jnp.bfloat16),
        scratch_shapes=[
            pltpu.VMEM((CHIP_EXPERTS, n, 4 * WIDTH), jnp.bfloat16),
            pltpu.VMEM((2, 2, 4, TILES * TOK, LANES), jnp.bfloat16),
            pltpu.VMEM((2, 4 * WIDTH, 2 * ff), jnp.bfloat16),
            pltpu.SemaphoreType.DMA((2, 8 * PARTS)),
            pltpu.SemaphoreType.DMA((2, 2)),
        ],
        compiler_params=pltpu.CompilerParams(vmem_limit_bytes=48 << 20),
        cost_estimate=pl.CostEstimate(
            flops=2 * 2048 * 4096 * 1024, bytes_accessed=100 << 20, transcendentals=2048 * 384
        ),
        name="hidden",
    )(place, groups, pick, weight, *flat, *own, *far)


def down_kernel(
    part, groups, place, put, hidden, d_own, d_far, low, high, weights, y, weight_sems
):
    tiles_in = tiles_of(part)
    f, begin = len(tiles_in) * LANES, tiles_in[0][0] * LANES

    def weight_copies(e):
        return [
            pltpu.make_async_copy(
                (d_own if e < 2 else d_far).at[e % 2, :, pl.ds(x * WIDTH + begin, f)],
                weights.at[e, :, pl.ds(x * f, f)],
                weight_sems.at[e, x],
            )
            for x in range(4)
        ]

    for e in range(CHIP_EXPERTS):
        for copy in weight_copies(e):
            copy.start()
    @pl.loop(0, CHIP_EXPERTS)
    def _(e):
        for x in range(4):
            to = weights.at[e, :, pl.ds(x * f, f)]
            pltpu.make_async_copy(d_own.at[0, :, pl.ds(begin, f)], to, weight_sems.at[e, x]).wait()

        @pl.loop(0, 2)
        def _(half):
            tiles = [pl.ds(pl.multiple_of((2 * half + i) * TILE, TILE), TILE) for i in range(2)]
            used = groups[e] > 2 * half

            @pl.when(used)
            def _():
                for tile in tiles:
                    for x in range(4):
                        cols = slice(x * f, (x + 1) * f)
                        value = jnp.dot(
                            hidden[e, tile], weights[e, :, cols], preferred_element_type=jnp.float32
                        )
                        y[e, tile, cols] = value.astype(jnp.bfloat16)

            @pl.when(jnp.logical_not(used))
            def _():
                for tile in tiles:
                    y[e, tile] = jnp.zeros((TILE, 4 * f), jnp.bfloat16)

    @pl.loop(0, PAIRS, unroll=2)
    def _(pair):
        at = pl.multiple_of(pair * GROUP_ROWS, GROUP_ROWS)
        for x in range(4):
            terms = [
                y[e, pl.ds(g * TILE + at, GROUP_ROWS), x * f : (x + 1) * f]
                for e in range(CHIP_EXPERTS)
                for g in range(GROUPS)
            ]
            terms = jnp.concatenate(terms, axis=0)
            total = jnp.dot(put[pair], terms, preferred_element_type=jnp.float32)
            total = total.astype(jnp.bfloat16)
            for blk in range(2):
                piece = [
                    total[blk * TOK + start : blk * TOK + stop, i * LANES : (i + 1) * LANES]
                    for i, (_, start, stop, _) in enumerate(tiles_in)
                ]
                piece = jnp.concatenate(piece, axis=0)
                j = place[part * PEERS + (2 * pair + blk) * 4 + x]
                low[jnp.minimum(j, HALF)] = piece
                high[jnp.where(j < HALF, HALF, j - HALF)] = piece


def find_sums(part, groups, place, put, hidden, own, far):
    f, ff = len(tiles_of(part)) * LANES, own.shape[1]
    n = BLOCKS * SLOTS
    anywhere = pl.BlockSpec(memory_space=pl.ANY)
    vmem = pl.BlockSpec(memory_space=pltpu.VMEM)
    smem = pl.BlockSpec(memory_space=pltpu.SMEM)
    return pl.pallas_call(
        functools.partial(down_kernel, part),
        in_specs=[smem, smem, vmem, vmem, anywhere, anywhere],
        out_specs=[vmem] * 2,
        out_shape=[jax.ShapeDtypeStruct((HALF + 1, ROWS[part], LANES), jnp.bfloat16)] * 2,
        scratch_shapes=[
            pltpu.VMEM((CHIP_EXPERTS, ff, 4 * f), jnp.bfloat16),
            pltpu.VMEM((CHIP_EXPERTS, n, 4 * f), jnp.bfloat16),
            pltpu.SemaphoreType.DMA((CHIP_EXPERTS, 4)),
        ],
        compiler_params=pltpu.CompilerParams(vmem_limit_bytes=32 << 20),
        cost_estimate=pl.CostEstimate(
            flops=2 * 2048 * 4 * f * (ff + 256), bytes_accessed=40 << 20, transcendentals=0
        ),
        name="sums",
    )(groups, place, put, hidden, own, far)


def routing(routes, core):
    mine = jnp.where(core == 0, routes, jnp.concatenate([routes[:, 2:], routes[:, :2]], axis=1))
    marked = mine > 0
    until = jnp.asarray(np.triu(np.ones((TOK, TOK), np.float32)), jnp.bfloat16)
    rank = jnp.einsum(
        "bes,st->bet", marked.astype(jnp.bfloat16), until, preferred_element_type=jnp.float32
    )
    rank = jnp.where(marked, rank.astype(jnp.int32) - 1, -1)
    groups = jnp.max(rank, axis=(0, 2)) // SLOT_STEP + 1
    row = np.arange(GROUPS * GROUP_ROWS)
    row_slot = row // GROUP_ROWS * SLOT_STEP + row % SLOT_STEP
    row_block = row % GROUP_ROWS // SLOT_STEP
    same = jnp.asarray(row_block[:, None] == np.arange(2 * TOK)[None, :] // TOK)

    def by_pair(v):
        v = v.reshape(PAIRS, 2, CHIP_EXPERTS, TOK).transpose(0, 2, 1, 3)
        return v.reshape(PAIRS, CHIP_EXPERTS, 1, 2 * TOK)

    chosen = (by_pair(rank) == jnp.asarray(row_slot, jnp.int32)[:, None]) & same
    slot_weight = jnp.sum(jnp.where(chosen, by_pair(mine), 0.0), axis=3)
    slot_weight = slot_weight.reshape(PAIRS, CHIP_EXPERTS, GROUPS, GROUP_ROWS)
    slot_weight = slot_weight.transpose(1, 2, 0, 3).reshape(CHIP_EXPERTS, BLOCKS * SLOTS, 1)
    pick = chosen.astype(jnp.bfloat16).reshape(PAIRS, PAIR_ROWS, 2 * TOK)
    put = pick.transpose(0, 2, 1)
    return groups, pick, put, slot_weight


def spread(tokens, weights, routes):
    tiled = tokens.reshape(TOK, TILES, LANES).transpose(1, 0, 2).reshape(TILES * TOK, LANES)
    held = [tiled[None, ROW_AT[p] : ROW_AT[p] + ROWS[p]] for p in range(PARTS)]
    weights, far = list(weights), []
    for stage in range(STAGES):
        if stage != 1 and len(far) < len(weights):
            far.append(lax.ppermute(weights[len(far)], AXES, core_pairs()))
        got = [lax.ppermute(held[p], AXES, stage_pairs(p, stage)) for p in range(PARTS)]
        if stage == STAGES - 1:
            return list(zip(held, got)), far, routes
        held = [jnp.concatenate([h, g], axis=0) for h, g in zip(held, got)]
        if 1 <= stage <= 2:
            held, far, weights = lax.optimization_barrier((held, far, weights))
        if stage == 3:
            held, far, routes = lax.optimization_barrier((held, far, routes))


def add(a, b):
    return (a.astype(jnp.float32) + b.astype(jnp.float32)).astype(jnp.bfloat16)


def collect(high, low, part):
    for stage in reversed(range(STAGES)):
        got = lax.ppermute(high, AXES, stage_pairs(part, stage))
        if stage:
            cut = 1 << (stage - 1)
            high = add(low[cut : 2 * cut], got[cut : 2 * cut])
            low = add(low[:cut], got[:cut])
    return low[0].astype(jnp.float32) + got[0].astype(jnp.float32)


def on_device(
    tokens, keep_mask, expert_ids, route_weight, w_gate, w_up, w_down, norm_gain, kv_weight
):
    y, z, c, x = (lax.axis_index(a) for a in AXES)
    me = ((y * 4 + z) * 2 + c) * 4 + x
    place = lax.dynamic_index_in_dim(jnp.asarray(place_table()), me, 0, keepdims=False)

    experts = CHIP_EXPERTS * BLOCKS
    live = (keep_mask > 0)[None, None, :]
    named = expert_ids.T[None] == jnp.arange(experts, dtype=jnp.int32)[:, None, None]
    routes = jnp.sum(jnp.where(named & live, route_weight.T[None], 0.0), axis=1)
    routes = routes.reshape(BLOCKS, CHIP_EXPERTS, TOK)
    routes = lax.all_to_all(routes, ("y", "z"), split_axis=0, concat_axis=0, tiled=True)
    own = (w_gate, w_up, w_down)
    pieces, far, routes = spread(tokens, own, routes)
    groups, pick, put, slot_weight = routing(routes, c)
    hidden = find_hidden(place, groups, pick, slot_weight, pieces, own[:2], far[:2])
    totals = []
    for part in range(PARTS):
        low, high = find_sums(part, groups, place, put, hidden, own[2], far[2])
        totals.append((high, low))
    summed = jnp.concatenate([collect(*totals[p], p) for p in range(PARTS)], axis=0)
    summed = summed.reshape(TILES, TOK, LANES).transpose(1, 0, 2).reshape(TOK, WIDTH)
    mixed_out = (tokens.astype(jnp.float32) + summed).astype(jnp.bfloat16)

    full = [mixed_out] + [lax.ppermute(mixed_out, AXES, x_pairs(m)) for m in (1, 2, 3)]
    full = jnp.concatenate(full, axis=1).astype(jnp.float32)
    order = [jnp.bitwise_xor(x, m) * WIDTH for m in range(4)]
    gain = jnp.concatenate([lax.dynamic_slice_in_dim(norm_gain, o, WIDTH) for o in order])
    kv = jnp.concatenate([lax.dynamic_slice_in_dim(kv_weight, o, WIDTH) for o in order])
    mean_square = jnp.mean(full * full, axis=-1, keepdims=True)
    normed = (full * lax.rsqrt(mean_square + 1e-06) * gain).astype(jnp.bfloat16)
    kv_rows = jnp.dot(normed, kv, preferred_element_type=jnp.float32).astype(jnp.bfloat16)
    return (mixed_out, kv_rows)


def solution(mesh):
    fine = Mesh(mesh.devices.reshape(SIZES), AXES)
    ep = ("y", "z", "c")
    in_specs = (
        P(ep, "x"),
        P(ep),
        P(ep, None),
        P(ep, None),
        P(ep, None, "x"),
        P(ep, None, "x"),
        P(ep, "x", None),
        P(),
        P(None, "x"),
    )
    out_specs = (P(ep, "x"), P(ep, "x"))
    return jax.shard_map(
        on_device, mesh=fine, in_specs=in_specs, out_specs=out_specs, check_vma=False
    )
```

```python
import functools

import jax
import jax.numpy as jnp
import numpy as np
from jax import lax
from jax.experimental import pallas as pl
from jax.experimental.pallas import tpu as pltpu
from jax.sharding import Mesh, PartitionSpec as P

AXES = ("y", "z", "c", "x")
SIZES = (4, 4, 2, 4)
LINKS = (("x", 1), ("y", 3), ("z", 1), ("x", 3), ("y", 1), ("z", 3))
STAGES = len(LINKS)
PEERS = 1 << STAGES
HALF = PEERS // 2
BLOCKS = 16
TOK = 128
WIDTH = 1024
SLOTS = 32
CHIP_EXPERTS = 4
LANES = 128
TILES = WIDTH // LANES
ROWS = (352, 336, 336)
ROW_AT = (0, 352, 688)
PARTS = len(ROWS)
BACK = (352, 336, 336)
BACK_AT = (0, 352, 688)
PAIRS = BLOCKS // 2
GROUPS = 4
AHEAD = 4
SLOT_STEP = SLOTS // GROUPS
GROUP_ROWS = 2 * SLOT_STEP
TILE = PAIRS * GROUP_ROWS
PAIR_ROWS = CHIP_EXPERTS * GROUPS * GROUP_ROWS


def tiles_of(part):
    first, last = BACK_AT[part], BACK_AT[part] + BACK[part]
    found = []
    for tile in range(first // TOK, -(-last // TOK)):
        start, stop = max(first - tile * TOK, 0), min(last - tile * TOK, TOK)
        found.append((tile, start, stop, tile * TOK + start - first))
    return found


def link_of(part, core, stage):
    return LINKS[(2 * part + 1 - core + stage) % STAGES]


def device_number(at):
    return ((at["y"] * 4 + at["z"]) * 2 + at["c"]) * 4 + at["x"]


def all_places():
    for y in range(4):
        for z in range(4):
            for c in range(2):
                for x in range(4):
                    yield dict(y=y, z=z, c=c, x=x)


def stage_pairs(part, stage):
    pairs = []
    for at in all_places():
        axis, mask = link_of(part, at["c"], stage)
        to = dict(at)
        to[axis] ^= mask
        pairs.append((device_number(at), device_number(to)))
    return pairs


def core_pairs():
    return [(device_number(at), device_number(dict(at, c=1 - at["c"]))) for at in all_places()]


def x_pairs(mask):
    return [(device_number(at), device_number(dict(at, x=at["x"] ^ mask))) for at in all_places()]


def place_table():
    place = np.zeros((128, PARTS, BLOCKS * 4), np.int32)
    for at in all_places():
        for part in range(PARTS):
            for j in range(PEERS):
                to = dict(at)
                for stage in range(STAGES):
                    if j >> stage & 1:
                        axis, mask = link_of(part, at["c"], stage)
                        to[axis] ^= mask
                place[device_number(at), part, (to["y"] * 4 + to["z"]) * 4 + to["x"]] = j
    return place.reshape(128, -1)


def hidden_kernel(
    place, groups, pick, weight, lo0, hi0, lo1, hi1, lo2, hi2, g_own, u_own, g_far, u_far,
    out, rows, tok, wide, tok_sems, weight_sems,
):
    low, high = (lo0, lo1, lo2), (hi0, hi1, hi2)
    ff = g_own.shape[2]

    def weight_copies(gate, up, at, slot):
        return (
            pltpu.make_async_copy(gate.at[at], wide.at[slot, :, pl.ds(0, ff)], weight_sems.at[slot, 0]),
            pltpu.make_async_copy(up.at[at], wide.at[slot, :, pl.ds(ff, ff)], weight_sems.at[slot, 1]),
        )

    def fetch(pair, slot, start):
        for blk in range(2):
            for x in range(4):
                for part in range(PARTS):
                    to = tok.at[slot, blk, x, pl.ds(ROW_AT[part], ROWS[part])]
                    sem = tok_sems.at[slot, (blk * 4 + x) * PARTS + part]
                    if not start:
                        pltpu.make_async_copy(low[part].at[0], to, sem).wait()
                        continue
                    j = place[part * PEERS + (2 * pair + blk) * 4 + x]

                    @pl.when(j < HALF)
                    def _(part=part, j=j, to=to, sem=sem):
                        pltpu.make_async_copy(low[part].at[j], to, sem).start()

                    @pl.when(j >= HALF)
                    def _(part=part, j=j, to=to, sem=sem):
                        pltpu.make_async_copy(high[part].at[j - HALF], to, sem).start()

    for pair in range(AHEAD - 1):
        fetch(pair, pair, True)
    for copy in weight_copies(g_own, u_own, 0, 0):
        copy.start()

    @pl.loop(0, PAIRS)
    def _(pair):
        slot = lax.rem(pair, AHEAD)

        @pl.when(pair + AHEAD - 1 < PAIRS)
        def _():
            fetch(pair + AHEAD - 1, lax.rem(pair + AHEAD - 1, AHEAD), True)

        fetch(pair, slot, False)
        at = pl.multiple_of(pair * GROUP_ROWS, GROUP_ROWS)
        for x in range(4):
            cols = slice(x * WIDTH, (x + 1) * WIDTH)
            held = [
                jnp.concatenate([tok[slot, blk, x, t * TOK : (t + 1) * TOK] for blk in range(2)], axis=0)
                for t in range(TILES)
            ]
            held = jnp.concatenate(held, axis=1)
            picked = jnp.dot(pick[pair], held, preferred_element_type=jnp.float32)
            picked = picked.astype(jnp.bfloat16)
            for e in range(CHIP_EXPERTS):
                for g in range(GROUPS):
                    first = (e * GROUPS + g) * GROUP_ROWS
                    rows[e, pl.ds(g * TILE + at, GROUP_ROWS), cols] = picked[first : first + GROUP_ROWS]

    for copy in weight_copies(g_own, u_own, 1, 1):
        copy.start()

    @pl.loop(0, CHIP_EXPERTS)
    def _(e):
        slot = lax.rem(e, 2)
        for copy in weight_copies(g_own, u_own, 0, slot):
            copy.wait()

        @pl.loop(0, lax.div(groups[e] + 1, 2))
        def _(g):
            for i in range(2):
                tile = pl.ds(pl.multiple_of((2 * g + i) * TILE, TILE), TILE)
                both = jnp.dot(rows[e, tile, :], wide[slot], preferred_element_type=jnp.float32)
                product = jax.nn.silu(both[:, :ff]) * both[:, ff:] * weight[e, tile]
                out[e, tile] = product.astype(jnp.bfloat16)

        @pl.when(e < 2)
        def _():
            for copy in weight_copies(g_far, u_far, e, slot):
                copy.start()


def find_hidden(place, groups, pick, weight, pieces, own, far):
    flat = [half for pair in pieces for half in pair]
    ff = own[0].shape[2]
    n = BLOCKS * SLOTS
    anywhere = pl.BlockSpec(memory_space=pl.ANY)
    vmem = pl.BlockSpec(memory_space=pltpu.VMEM)
    smem = pl.BlockSpec(memory_space=pltpu.SMEM)
    return pl.pallas_call(
        hidden_kernel,
        in_specs=[smem, smem, vmem, vmem] + [anywhere] * 10,
        out_specs=vmem,
        out_shape=jax.ShapeDtypeStruct((CHIP_EXPERTS, n, ff), jnp.bfloat16),
        scratch_shapes=[
            pltpu.VMEM((CHIP_EXPERTS, n, 4 * WIDTH), jnp.bfloat16),
            pltpu.VMEM((AHEAD, 2, 4, TILES * TOK, LANES), jnp.bfloat16),
            pltpu.VMEM((2, 4 * WIDTH, 2 * ff), jnp.bfloat16),
            pltpu.SemaphoreType.DMA((AHEAD, 8 * PARTS)),
            pltpu.SemaphoreType.DMA((2, 2)),
        ],
        compiler_params=pltpu.CompilerParams(vmem_limit_bytes=44 << 20),
        cost_estimate=pl.CostEstimate(
            flops=2 * 2048 * 4096 * 1024, bytes_accessed=100 << 20, transcendentals=2048 * 384
        ),
        name="hidden",
    )(place, groups, pick, weight, *flat, *own, *far)


def down_kernel(
    part, groups, place, put, hidden, d_own, d_far, low, high, weights, y, weight_sems
):
    tiles_in = tiles_of(part)
    f, begin = len(tiles_in) * LANES, tiles_in[0][0] * LANES

    def weight_copies(e):
        return [
            pltpu.make_async_copy(
                (d_own if e < 2 else d_far).at[e % 2, :, pl.ds(x * WIDTH + begin, f)],
                weights.at[e, :, pl.ds(x * f, f)],
                weight_sems.at[e, x],
            )
            for x in range(4)
        ]

    for e in range(CHIP_EXPERTS):
        for copy in weight_copies(e):
            copy.start()
    @pl.loop(0, CHIP_EXPERTS)
    def _(e):
        for x in range(4):
            to = weights.at[e, :, pl.ds(x * f, f)]
            pltpu.make_async_copy(d_own.at[0, :, pl.ds(begin, f)], to, weight_sems.at[e, x]).wait()

        @pl.loop(0, 2)
        def _(half):
            tiles = [pl.ds(pl.multiple_of((2 * half + i) * TILE, TILE), TILE) for i in range(2)]
            used = groups[e] > 2 * half

            @pl.when(used)
            def _():
                for tile in tiles:
                    for x in range(4):
                        cols = slice(x * f, (x + 1) * f)
                        value = jnp.dot(
                            hidden[e, tile], weights[e, :, cols], preferred_element_type=jnp.float32
                        )
                        y[e, tile, cols] = value.astype(jnp.bfloat16)

            @pl.when(jnp.logical_not(used))
            def _():
                for tile in tiles:
                    y[e, tile] = jnp.zeros((TILE, 4 * f), jnp.bfloat16)

    @pl.loop(0, PAIRS, unroll=2)
    def _(pair):
        at = pl.multiple_of(pair * GROUP_ROWS, GROUP_ROWS)
        for x in range(4):
            terms = [
                y[e, pl.ds(g * TILE + at, GROUP_ROWS), x * f : (x + 1) * f]
                for e in range(CHIP_EXPERTS)
                for g in range(GROUPS)
            ]
            terms = jnp.concatenate(terms, axis=0)
            total = jnp.dot(put[pair], terms, preferred_element_type=jnp.float32)
            total = total.astype(jnp.bfloat16)
            for blk in range(2):
                piece = [
                    total[blk * TOK + start : blk * TOK + stop, i * LANES : (i + 1) * LANES]
                    for i, (_, start, stop, _) in enumerate(tiles_in)
                ]
                piece = jnp.concatenate(piece, axis=0)
                j = place[part * PEERS + (2 * pair + blk) * 4 + x]
                low[jnp.minimum(j, HALF)] = piece
                high[jnp.where(j < HALF, HALF, j - HALF)] = piece


def find_sums(part, groups, place, put, hidden, own, far):
    f, ff = len(tiles_of(part)) * LANES, own.shape[1]
    n = BLOCKS * SLOTS
    anywhere = pl.BlockSpec(memory_space=pl.ANY)
    vmem = pl.BlockSpec(memory_space=pltpu.VMEM)
    smem = pl.BlockSpec(memory_space=pltpu.SMEM)
    return pl.pallas_call(
        functools.partial(down_kernel, part),
        in_specs=[smem, smem, vmem, vmem, anywhere, anywhere],
        out_specs=[vmem] * 2,
        out_shape=[jax.ShapeDtypeStruct((HALF + 1, BACK[part], LANES), jnp.bfloat16)] * 2,
        scratch_shapes=[
            pltpu.VMEM((CHIP_EXPERTS, ff, 4 * f), jnp.bfloat16),
            pltpu.VMEM((CHIP_EXPERTS, n, 4 * f), jnp.bfloat16),
            pltpu.SemaphoreType.DMA((CHIP_EXPERTS, 4)),
        ],
        compiler_params=pltpu.CompilerParams(vmem_limit_bytes=28 << 20),
        cost_estimate=pl.CostEstimate(
            flops=2 * 2048 * 4 * f * (ff + 256), bytes_accessed=40 << 20, transcendentals=0
        ),
        name="sums",
    )(groups, place, put, hidden, own, far)


def routing(routes, core):
    mine = jnp.where(core == 0, routes, jnp.concatenate([routes[:, 2:], routes[:, :2]], axis=1))
    marked = mine > 0
    until = jnp.asarray(np.triu(np.ones((TOK, TOK), np.float32)), jnp.bfloat16)
    rank = jnp.einsum(
        "bes,st->bet", marked.astype(jnp.bfloat16), until, preferred_element_type=jnp.float32
    )
    rank = jnp.where(marked, rank.astype(jnp.int32) - 1, -1)
    groups = jnp.max(rank, axis=(0, 2)) // SLOT_STEP + 1
    row = np.arange(GROUPS * GROUP_ROWS)
    row_slot = row // GROUP_ROWS * SLOT_STEP + row % SLOT_STEP
    row_block = row % GROUP_ROWS // SLOT_STEP
    same = jnp.asarray(row_block[:, None] == np.arange(2 * TOK)[None, :] // TOK)

    def by_pair(v):
        v = v.reshape(PAIRS, 2, CHIP_EXPERTS, TOK).transpose(0, 2, 1, 3)
        return v.reshape(PAIRS, CHIP_EXPERTS, 1, 2 * TOK)

    chosen = (by_pair(rank) == jnp.asarray(row_slot, jnp.int32)[:, None]) & same
    slot_weight = jnp.sum(jnp.where(chosen, by_pair(mine), 0.0), axis=3)
    slot_weight = slot_weight.reshape(PAIRS, CHIP_EXPERTS, GROUPS, GROUP_ROWS)
    slot_weight = slot_weight.transpose(1, 2, 0, 3).reshape(CHIP_EXPERTS, BLOCKS * SLOTS, 1)
    pick = chosen.astype(jnp.bfloat16).reshape(PAIRS, PAIR_ROWS, 2 * TOK)
    put = pick.transpose(0, 2, 1)
    return groups, pick, put, slot_weight


def spread(tokens, weights, routes):
    tiled = tokens.reshape(TOK, TILES, LANES).transpose(1, 0, 2).reshape(TILES * TOK, LANES)
    held = [tiled[None, ROW_AT[p] : ROW_AT[p] + ROWS[p]] for p in range(PARTS)]
    weights, far = list(weights), []
    for stage in range(STAGES):
        if stage != 1 and len(far) < len(weights):
            far.append(lax.ppermute(weights[len(far)], AXES, core_pairs()))
        got = [lax.ppermute(held[p], AXES, stage_pairs(p, stage)) for p in range(PARTS)]
        if stage == STAGES - 1:
            return list(zip(held, got)), far, routes
        held = [jnp.concatenate([h, g], axis=0) for h, g in zip(held, got)]
        if 1 <= stage <= 2:
            held, far, weights = lax.optimization_barrier((held, far, weights))
        if stage == 3:
            held, far, routes = lax.optimization_barrier((held, far, routes))


def add(a, b):
    return (a.astype(jnp.float32) + b.astype(jnp.float32)).astype(jnp.bfloat16)


def collect(high, low, part):
    for stage in reversed(range(STAGES)):
        got = lax.ppermute(high, AXES, stage_pairs(part, stage))
        if stage:
            cut = 1 << (stage - 1)
            high = add(low[cut : 2 * cut], got[cut : 2 * cut])
            low = add(low[:cut], got[:cut])
    return low[0].astype(jnp.float32) + got[0].astype(jnp.float32)


def on_device(
    tokens, keep_mask, expert_ids, route_weight, w_gate, w_up, w_down, norm_gain, kv_weight
):
    y, z, c, x = (lax.axis_index(a) for a in AXES)
    me = ((y * 4 + z) * 2 + c) * 4 + x
    place = lax.dynamic_index_in_dim(jnp.asarray(place_table()), me, 0, keepdims=False)

    experts = CHIP_EXPERTS * BLOCKS
    live = (keep_mask > 0)[None, None, :]
    named = expert_ids.T[None] == jnp.arange(experts, dtype=jnp.int32)[:, None, None]
    routes = jnp.sum(jnp.where(named & live, route_weight.T[None], 0.0), axis=1)
    routes = routes.reshape(BLOCKS, CHIP_EXPERTS, TOK)
    routes = lax.all_to_all(routes, ("y", "z"), split_axis=0, concat_axis=0, tiled=True)
    own = (w_gate, w_up, w_down)
    pieces, far, routes = spread(tokens, own, routes)
    groups, pick, put, slot_weight = routing(routes, c)
    hidden = find_hidden(place, groups, pick, slot_weight, pieces, own[:2], far[:2])
    totals = []
    for part in range(PARTS):
        low, high = find_sums(part, groups, place, put, hidden, own[2], far[2])
        totals.append((high, low))
    summed = jnp.concatenate([collect(*totals[p], p) for p in range(PARTS)], axis=0)
    summed = summed.reshape(TILES, TOK, LANES).transpose(1, 0, 2).reshape(TOK, WIDTH)
    mixed_out = (tokens.astype(jnp.float32) + summed).astype(jnp.bfloat16)

    full = [mixed_out] + [lax.ppermute(mixed_out, AXES, x_pairs(m)) for m in (1, 2, 3)]
    full = jnp.concatenate(full, axis=1).astype(jnp.float32)
    order = [jnp.bitwise_xor(x, m) * WIDTH for m in range(4)]
    gain = jnp.concatenate([lax.dynamic_slice_in_dim(norm_gain, o, WIDTH) for o in order])
    kv = jnp.concatenate([lax.dynamic_slice_in_dim(kv_weight, o, WIDTH) for o in order])
    mean_square = jnp.mean(full * full, axis=-1, keepdims=True)
    normed = (full * lax.rsqrt(mean_square + 1e-06) * gain).astype(jnp.bfloat16)
    kv_rows = jnp.dot(normed, kv, preferred_element_type=jnp.float32).astype(jnp.bfloat16)
    return (mixed_out, kv_rows)


def solution(mesh):
    fine = Mesh(mesh.devices.reshape(SIZES), AXES)
    ep = ("y", "z", "c")
    in_specs = (
        P(ep, "x"),
        P(ep),
        P(ep, None),
        P(ep, None),
        P(ep, None, "x"),
        P(ep, None, "x"),
        P(ep, "x", None),
        P(),
        P(None, "x"),
    )
    out_specs = (P(ep, "x"), P(ep, "x"))
    return jax.shard_map(
        on_device, mesh=fine, in_specs=in_specs, out_specs=out_specs, check_vma=False
    )
```

```python
import functools

import jax
import jax.numpy as jnp
import numpy as np
from jax import lax
from jax.experimental import pallas as pl
from jax.experimental.pallas import tpu as pltpu
from jax.sharding import Mesh, PartitionSpec as P

AXES = ("y", "z", "c", "x")
SIZES = (4, 4, 2, 4)
LINKS = (("x", 1), ("y", 3), ("z", 1), ("x", 3), ("y", 1), ("z", 3))
STAGES = len(LINKS)
PEERS = 1 << STAGES
HALF = PEERS // 2
BLOCKS = 16
TOK = 128
WIDTH = 1024
SLOTS = 32
CHIP_EXPERTS = 4
LANES = 128
TILES = WIDTH // LANES
ROWS = (352, 336, 336)
ROW_AT = (0, 352, 688)
PARTS = len(ROWS)
BACK = (352, 336, 336)
BACK_AT = (0, 352, 688)
PAIRS = BLOCKS // 2
GROUPS = 4
AHEAD = 4
SLOT_STEP = SLOTS // GROUPS
GROUP_ROWS = 2 * SLOT_STEP
TILE = PAIRS * GROUP_ROWS
PAIR_ROWS = CHIP_EXPERTS * GROUPS * GROUP_ROWS


def tiles_of(part):
    first, last = BACK_AT[part], BACK_AT[part] + BACK[part]
    found = []
    for tile in range(first // TOK, -(-last // TOK)):
        start, stop = max(first - tile * TOK, 0), min(last - tile * TOK, TOK)
        found.append((tile, start, stop, tile * TOK + start - first))
    return found


def link_of(part, core, stage):
    return LINKS[(2 * part + 1 - core + stage) % STAGES]


def device_number(at):
    return ((at["y"] * 4 + at["z"]) * 2 + at["c"]) * 4 + at["x"]


def all_places():
    for y in range(4):
        for z in range(4):
            for c in range(2):
                for x in range(4):
                    yield dict(y=y, z=z, c=c, x=x)


def stage_pairs(part, stage):
    pairs = []
    for at in all_places():
        axis, mask = link_of(part, at["c"], stage)
        to = dict(at)
        to[axis] ^= mask
        pairs.append((device_number(at), device_number(to)))
    return pairs


def core_pairs():
    return [(device_number(at), device_number(dict(at, c=1 - at["c"]))) for at in all_places()]


def x_pairs(mask):
    return [(device_number(at), device_number(dict(at, x=at["x"] ^ mask))) for at in all_places()]


def place_table():
    place = np.zeros((128, PARTS, BLOCKS * 4), np.int32)
    for at in all_places():
        for part in range(PARTS):
            for j in range(PEERS):
                to = dict(at)
                for stage in range(STAGES):
                    if j >> stage & 1:
                        axis, mask = link_of(part, at["c"], stage)
                        to[axis] ^= mask
                place[device_number(at), part, (to["y"] * 4 + to["z"]) * 4 + to["x"]] = j
    return place.reshape(128, -1)


def hidden_kernel(
    place, groups, pick, weight, lo0, hi0, lo1, hi1, lo2, hi2, g_own, u_own, g_far, u_far,
    out, rows, tok, wide, tok_sems, weight_sems,
):
    low, high = (lo0, lo1, lo2), (hi0, hi1, hi2)
    ff = g_own.shape[2]

    def weight_copies(gate, up, at, slot):
        return (
            pltpu.make_async_copy(gate.at[at], wide.at[slot, :, pl.ds(0, ff)], weight_sems.at[slot, 0]),
            pltpu.make_async_copy(up.at[at], wide.at[slot, :, pl.ds(ff, ff)], weight_sems.at[slot, 1]),
        )

    def fetch(pair, slot, start):
        for blk in range(2):
            for x in range(4):
                for part in range(PARTS):
                    to = tok.at[slot, blk, x, pl.ds(ROW_AT[part], ROWS[part])]
                    sem = tok_sems.at[slot, (blk * 4 + x) * PARTS + part]
                    if not start:
                        pltpu.make_async_copy(low[part].at[0], to, sem).wait()
                        continue
                    j = place[part * PEERS + (2 * pair + blk) * 4 + x]

                    @pl.when(j < HALF)
                    def _(part=part, j=j, to=to, sem=sem):
                        pltpu.make_async_copy(low[part].at[j], to, sem).start()

                    @pl.when(j >= HALF)
                    def _(part=part, j=j, to=to, sem=sem):
                        pltpu.make_async_copy(high[part].at[j - HALF], to, sem).start()

    for pair in range(AHEAD - 1):
        fetch(pair, pair, True)
    for copy in weight_copies(g_own, u_own, 0, 0):
        copy.start()

    @pl.loop(0, PAIRS)
    def _(pair):
        slot = lax.rem(pair, AHEAD)

        @pl.when(pair + AHEAD - 1 < PAIRS)
        def _():
            fetch(pair + AHEAD - 1, lax.rem(pair + AHEAD - 1, AHEAD), True)

        fetch(pair, slot, False)
        at = pl.multiple_of(pair * GROUP_ROWS, GROUP_ROWS)
        for x in range(4):
            cols = slice(x * WIDTH, (x + 1) * WIDTH)
            held = [
                jnp.concatenate([tok[slot, blk, x, t * TOK : (t + 1) * TOK] for blk in range(2)], axis=0)
                for t in range(TILES)
            ]
            held = jnp.concatenate(held, axis=1)
            picked = jnp.dot(pick[pair], held, preferred_element_type=jnp.float32)
            picked = picked.astype(jnp.bfloat16)
            for e in range(CHIP_EXPERTS):
                for g in range(GROUPS):
                    first = (e * GROUPS + g) * GROUP_ROWS
                    rows[e, pl.ds(g * TILE + at, GROUP_ROWS), cols] = picked[first : first + GROUP_ROWS]

    for copy in weight_copies(g_own, u_own, 1, 1):
        copy.start()

    @pl.loop(0, CHIP_EXPERTS)
    def _(e):
        slot = lax.rem(e, 2)
        for copy in weight_copies(g_own, u_own, 0, slot):
            copy.wait()

        @pl.loop(0, lax.div(groups[e] + 1, 2))
        def _(g):
            for i in range(2):
                tile = pl.ds(pl.multiple_of((2 * g + i) * TILE, TILE), TILE)
                both = jnp.dot(rows[e, tile, :], wide[slot], preferred_element_type=jnp.float32)
                product = jax.nn.silu(both[:, :ff]) * both[:, ff:] * weight[e, tile]
                out[e, tile] = product.astype(jnp.bfloat16)

        @pl.when(e < 2)
        def _():
            for copy in weight_copies(g_far, u_far, e, slot):
                copy.start()


def find_hidden(place, groups, pick, weight, pieces, own, far):
    flat = [half for pair in pieces for half in pair]
    ff = own[0].shape[2]
    n = BLOCKS * SLOTS
    anywhere = pl.BlockSpec(memory_space=pl.ANY)
    vmem = pl.BlockSpec(memory_space=pltpu.VMEM)
    smem = pl.BlockSpec(memory_space=pltpu.SMEM)
    return pl.pallas_call(
        hidden_kernel,
        in_specs=[smem, smem, vmem, vmem] + [anywhere] * 10,
        out_specs=vmem,
        out_shape=jax.ShapeDtypeStruct((CHIP_EXPERTS, n, ff), jnp.bfloat16),
        scratch_shapes=[
            pltpu.VMEM((CHIP_EXPERTS, n, 4 * WIDTH), jnp.bfloat16),
            pltpu.VMEM((AHEAD, 2, 4, TILES * TOK, LANES), jnp.bfloat16),
            pltpu.VMEM((2, 4 * WIDTH, 2 * ff), jnp.bfloat16),
            pltpu.SemaphoreType.DMA((AHEAD, 8 * PARTS)),
            pltpu.SemaphoreType.DMA((2, 2)),
        ],
        compiler_params=pltpu.CompilerParams(vmem_limit_bytes=44 << 20),
        cost_estimate=pl.CostEstimate(
            flops=2 * 2048 * 4096 * 1024, bytes_accessed=100 << 20, transcendentals=2048 * 384
        ),
        name="hidden",
    )(place, groups, pick, weight, *flat, *own, *far)


def down_kernel(
    part, groups, place, put, hidden, d_own, d_far, low, high, weights, y, weight_sems
):
    tiles_in = tiles_of(part)
    f, begin = len(tiles_in) * LANES, tiles_in[0][0] * LANES

    def weight_copies(e):
        return [
            pltpu.make_async_copy(
                (d_own if e < 2 else d_far).at[e % 2, :, pl.ds(x * WIDTH + begin, f)],
                weights.at[e, :, pl.ds(x * f, f)],
                weight_sems.at[e, x],
            )
            for x in range(4)
        ]

    for e in range(CHIP_EXPERTS):
        for copy in weight_copies(e):
            copy.start()
    @pl.loop(0, CHIP_EXPERTS)
    def _(e):
        for x in range(4):
            to = weights.at[e, :, pl.ds(x * f, f)]
            pltpu.make_async_copy(d_own.at[0, :, pl.ds(begin, f)], to, weight_sems.at[e, x]).wait()

        @pl.loop(0, 2)
        def _(half):
            tiles = [pl.ds(pl.multiple_of((2 * half + i) * TILE, TILE), TILE) for i in range(2)]
            used = groups[e] > 2 * half

            @pl.when(used)
            def _():
                for tile in tiles:
                    for x in range(4):
                        cols = slice(x * f, (x + 1) * f)
                        value = jnp.dot(
                            hidden[e, tile], weights[e, :, cols], preferred_element_type=jnp.float32
                        )
                        y[e, tile, cols] = value.astype(jnp.bfloat16)

            @pl.when(jnp.logical_not(used))
            def _():
                for tile in tiles:
                    y[e, tile] = jnp.zeros((TILE, 4 * f), jnp.bfloat16)

    @pl.loop(0, PAIRS, unroll=2)
    def _(pair):
        at = pl.multiple_of(pair * GROUP_ROWS, GROUP_ROWS)
        for x in range(4):
            terms = [
                y[e, pl.ds(g * TILE + at, GROUP_ROWS), x * f : (x + 1) * f]
                for e in range(CHIP_EXPERTS)
                for g in range(GROUPS)
            ]
            terms = jnp.concatenate(terms, axis=0)
            total = jnp.dot(put[pair], terms, preferred_element_type=jnp.float32)
            total = total.astype(jnp.bfloat16)
            for blk in range(2):
                piece = [
                    total[blk * TOK + start : blk * TOK + stop, i * LANES : (i + 1) * LANES]
                    for i, (_, start, stop, _) in enumerate(tiles_in)
                ]
                piece = jnp.concatenate(piece, axis=0)
                j = place[part * PEERS + (2 * pair + blk) * 4 + x]
                low[jnp.minimum(j, HALF)] = piece
                high[jnp.where(j < HALF, HALF, j - HALF)] = piece


def find_sums(part, groups, place, put, hidden, own, far):
    f, ff = len(tiles_of(part)) * LANES, own.shape[1]
    n = BLOCKS * SLOTS
    anywhere = pl.BlockSpec(memory_space=pl.ANY)
    vmem = pl.BlockSpec(memory_space=pltpu.VMEM)
    smem = pl.BlockSpec(memory_space=pltpu.SMEM)
    return pl.pallas_call(
        functools.partial(down_kernel, part),
        in_specs=[smem, smem, vmem, vmem, anywhere, anywhere],
        out_specs=[vmem] * 2,
        out_shape=[jax.ShapeDtypeStruct((HALF + 1, BACK[part], LANES), jnp.bfloat16)] * 2,
        scratch_shapes=[
            pltpu.VMEM((CHIP_EXPERTS, ff, 4 * f), jnp.bfloat16),
            pltpu.VMEM((CHIP_EXPERTS, n, 4 * f), jnp.bfloat16),
            pltpu.SemaphoreType.DMA((CHIP_EXPERTS, 4)),
        ],
        compiler_params=pltpu.CompilerParams(vmem_limit_bytes=28 << 20),
        cost_estimate=pl.CostEstimate(
            flops=2 * 2048 * 4 * f * (ff + 256), bytes_accessed=40 << 20, transcendentals=0
        ),
        name="sums",
    )(groups, place, put, hidden, own, far)


def routing(routes, core):
    mine = jnp.where(core == 0, routes, jnp.concatenate([routes[:, 2:], routes[:, :2]], axis=1))
    marked = mine > 0
    until = jnp.asarray(np.triu(np.ones((TOK, TOK), np.float32)), jnp.bfloat16)
    rank = jnp.einsum(
        "bes,st->bet", marked.astype(jnp.bfloat16), until, preferred_element_type=jnp.float32
    )
    rank = jnp.where(marked, rank.astype(jnp.int32) - 1, -1)
    groups = jnp.max(rank, axis=(0, 2)) // SLOT_STEP + 1
    row = np.arange(GROUPS * GROUP_ROWS)
    row_slot = row // GROUP_ROWS * SLOT_STEP + row % SLOT_STEP
    row_block = row % GROUP_ROWS // SLOT_STEP
    same = jnp.asarray(row_block[:, None] == np.arange(2 * TOK)[None, :] // TOK)

    def by_pair(v):
        v = v.reshape(PAIRS, 2, CHIP_EXPERTS, TOK).transpose(0, 2, 1, 3)
        return v.reshape(PAIRS, CHIP_EXPERTS, 1, 2 * TOK)

    chosen = (by_pair(rank) == jnp.asarray(row_slot, jnp.int32)[:, None]) & same
    slot_weight = jnp.sum(jnp.where(chosen, by_pair(mine), 0.0), axis=3)
    slot_weight = slot_weight.reshape(PAIRS, CHIP_EXPERTS, GROUPS, GROUP_ROWS)
    slot_weight = slot_weight.transpose(1, 2, 0, 3).reshape(CHIP_EXPERTS, BLOCKS * SLOTS, 1)
    pick = chosen.astype(jnp.bfloat16).reshape(PAIRS, PAIR_ROWS, 2 * TOK)
    put = pick.transpose(0, 2, 1)
    return groups, pick, put, slot_weight


def spread(tokens, weights, routes):
    tiled = tokens.reshape(TOK, TILES, LANES).transpose(1, 0, 2).reshape(TILES * TOK, LANES)
    held = [tiled[None, ROW_AT[p] : ROW_AT[p] + ROWS[p]] for p in range(PARTS)]
    weights, far = list(weights), []
    for stage in range(STAGES):
        if stage != 1 and len(far) < len(weights):
            far.append(lax.ppermute(weights[len(far)], AXES, core_pairs()))
        got = [lax.ppermute(held[p], AXES, stage_pairs(p, stage)) for p in range(PARTS)]
        if stage == STAGES - 1:
            return list(zip(held, got)), far, routes
        held = [jnp.concatenate([h, g], axis=0) for h, g in zip(held, got)]
        if stage == 2:
            held, far, weights = lax.optimization_barrier((held, far, weights))
        if stage == 3:
            held, far, routes = lax.optimization_barrier((held, far, routes))


def add(a, b):
    return (a.astype(jnp.float32) + b.astype(jnp.float32)).astype(jnp.bfloat16)


def collect(high, low, part):
    for stage in reversed(range(STAGES)):
        got = lax.ppermute(high, AXES, stage_pairs(part, stage))
        if stage:
            cut = 1 << (stage - 1)
            high = add(low[cut : 2 * cut], got[cut : 2 * cut])
            low = add(low[:cut], got[:cut])
    return low[0].astype(jnp.float32) + got[0].astype(jnp.float32)


def on_device(
    tokens, keep_mask, expert_ids, route_weight, w_gate, w_up, w_down, norm_gain, kv_weight
):
    y, z, c, x = (lax.axis_index(a) for a in AXES)
    me = ((y * 4 + z) * 2 + c) * 4 + x
    place = lax.dynamic_index_in_dim(jnp.asarray(place_table()), me, 0, keepdims=False)

    experts = CHIP_EXPERTS * BLOCKS
    live = (keep_mask > 0)[None, None, :]
    named = expert_ids.T[None] == jnp.arange(experts, dtype=jnp.int32)[:, None, None]
    routes = jnp.sum(jnp.where(named & live, route_weight.T[None], 0.0), axis=1)
    routes = routes.reshape(BLOCKS, CHIP_EXPERTS, TOK)
    routes = lax.all_to_all(routes, ("y", "z"), split_axis=0, concat_axis=0, tiled=True)
    own = (w_gate, w_up, w_down)
    pieces, far, routes = spread(tokens, own, routes)
    groups, pick, put, slot_weight = routing(routes, c)
    hidden = find_hidden(place, groups, pick, slot_weight, pieces, own[:2], far[:2])
    totals = []
    for part in range(PARTS):
        low, high = find_sums(part, groups, place, put, hidden, own[2], far[2])
        totals.append((high, low))
    summed = jnp.concatenate([collect(*totals[p], p) for p in range(PARTS)], axis=0)
    summed = summed.reshape(TILES, TOK, LANES).transpose(1, 0, 2).reshape(TOK, WIDTH)
    mixed_out = (tokens.astype(jnp.float32) + summed).astype(jnp.bfloat16)

    full = [mixed_out] + [lax.ppermute(mixed_out, AXES, x_pairs(m)) for m in (1, 2, 3)]
    full = jnp.concatenate(full, axis=1).astype(jnp.float32)
    order = [jnp.bitwise_xor(x, m) * WIDTH for m in range(4)]
    gain = jnp.concatenate([lax.dynamic_slice_in_dim(norm_gain, o, WIDTH) for o in order])
    kv = jnp.concatenate([lax.dynamic_slice_in_dim(kv_weight, o, WIDTH) for o in order])
    mean_square = jnp.mean(full * full, axis=-1, keepdims=True)
    normed = (full * lax.rsqrt(mean_square + 1e-06) * gain).astype(jnp.bfloat16)
    kv_rows = jnp.dot(normed, kv, preferred_element_type=jnp.float32).astype(jnp.bfloat16)
    return (mixed_out, kv_rows)


def solution(mesh):
    fine = Mesh(mesh.devices.reshape(SIZES), AXES)
    ep = ("y", "z", "c")
    in_specs = (
        P(ep, "x"),
        P(ep),
        P(ep, None),
        P(ep, None),
        P(ep, None, "x"),
        P(ep, None, "x"),
        P(ep, "x", None),
        P(),
        P(None, "x"),
    )
    out_specs = (P(ep, "x"), P(ep, "x"))
    return jax.shard_map(
        on_device, mesh=fine, in_specs=in_specs, out_specs=out_specs, check_vma=False
    )
```
